512 devices in a mesh: gx: 32 (over z, x), gy: 16 (over y, core).
Axes of the slice: x: 4, y: 8, z: 8, core: 2. Of those that a mesh axis runs over, the one named last changes fastest.
Arguments:
- field: float32 [512, 256, 128], P('gx', 'gy'), may hold values from -6 to 6
- conductance: float32 [512, 256, 128], P('gx', 'gy'), may hold values from 200 to 5000
- source: float32 [512, 256, 128], P('gx', 'gy'), may hold values from -600 to 600
Outputs:
- advanced: float32 [512, 256, 128], P('gx', 'gy')
The draws below stay inside these ranges and needn't reach their ends.
All inputs are finite; a program needn't handle non-finite values.
Results may differ from the reference program's by a relative error of at most 0.0003.
Values sent between devices are 32-bit elements; how exact they have to be, the bound alone decides.
No kernel may reach another device: no remote copies, remote signals or barrier semaphores. Data moves between devices by JAX's collectives and lax.ppermute only.
A program may use at most 64 MiB of HBM per device.

```python
import math
import jax
import jax.numpy as jnp
from jax import lax

NZ = 128
NX = 512
NY = 256


def shard_levels(rng, extent, shards, smallest, top_value):
    gain, own = 1.0, jax.random.fold_in(rng, 6)
    for position, shards_of in shards:
        steps = jnp.exp(jax.random.uniform(jax.random.fold_in(own, position), (shards_of,), jnp.float32, smallest / len(shards), top_value / len(shards)))
        gain = gain * jnp.repeat(steps, extent[position] // shards_of).reshape([-1 if axis == position else 1 for axis in range(len(extent))])
    return gain


def bell_draw(own_key, extent, spread, reach, split=(), dtype=jnp.bfloat16):
    factor_of = shard_levels(own_key, extent, split, -0.22, 0.18) if split else 1.0
    drawn = jax.random.normal(own_key, extent, jnp.float32) * spread * factor_of
    return jnp.minimum(jnp.maximum(drawn, -reach), reach).astype(dtype)


def setup_inputs(seed: int = 0) -> dict:
    key_of = jax.random.split(jax.random.key(seed), 4)
    return {
        "field": bell_draw(key_of[0], (NX, NY, NZ), 1.0, 6.0, ((0, 32), (1, 16)), jnp.float32),
        "conductance": jnp.clip(jnp.exp(math.log(5000.0) - 3.218876 * jax.random.uniform(key_of[1], (NX, NY, NZ), jnp.float32) ** shard_levels(key_of[1], (NX, NY, NZ), ((0, 32), (1, 16)), -0.2, 0.2)), 200.0, 5000.0),
        "source": bell_draw(key_of[2], (NX, NY, NZ), 100.0, 600.0, ((0, 32), (1, 16)), jnp.float32),
    }


def face_coeffs(cond):
    padded = jnp.pad(cond, ((1, 1), (0, 0), (0, 0)))
    return 0.5 * (padded[:-1] + padded[1:])

def apply_front(values, cond):
    faces = face_coeffs(cond)
    padded = jnp.pad(values, ((1, 1), (0, 0), (0, 0)))
    flux = faces * (padded[1:] - padded[:-1])
    return flux[1:] - flux[:-1]

def apply_along(values, cond, axis):
    moved = apply_front(jnp.moveaxis(values, axis, 0), jnp.moveaxis(cond, axis, 0))
    return jnp.moveaxis(moved, 0, axis)

def solve_along(rights, cond, axis):
    faces = face_coeffs(jnp.moveaxis(cond, axis, 0))
    lower = -0.5 * faces[:-1]
    upper = -0.5 * faces[1:]
    diag = 1.0 - lower - upper
    lower = lower.at[0].set(0.0)
    upper = upper.at[-1].set(0.0)
    moved = jnp.moveaxis(jnp.moveaxis(rights, axis, 0), 0, -1)
    solved = lax.linalg.tridiagonal_solve(jnp.moveaxis(lower, 0, -1), jnp.moveaxis(diag, 0, -1), jnp.moveaxis(upper, 0, -1), moved[..., None])[..., 0]
    return jnp.moveaxis(jnp.moveaxis(solved, -1, 0), 0, axis)

def reference(field, conductance, source):
    apply_x = apply_along(field, conductance, 0)
    apply_y = apply_along(field, conductance, 1)
    apply_z = apply_along(field, conductance, 2)
    first = field + 0.5 * apply_x + apply_y + apply_z + source
    section_x = solve_along(first, conductance, 0)
    section_y = solve_along(section_x - 0.5 * apply_y, conductance, 1)
    return solve_along(section_y - 0.5 * apply_z, conductance, 2)
```

```python
import jax
import jax.numpy as jnp
from jax import lax
from jax.experimental import pallas as pl
from jax.experimental.pallas import tpu as pltpu
from jax.sharding import PartitionSpec as P

N = 16
LANES = 128
ROUNDS = (1, 2, 4, 8, 16, 32, 64)
VALUES = 8


def rows(k):
    return pl.ds(N * k, N)


def turned(k):
    return pl.ds(k, N, stride=N)


def shape(*dims):
    return jax.ShapeDtypeStruct(dims, jnp.float32)


def eliminated(cells, emit):
    one = jnp.ones_like(cells[0])
    half = [None] + [0.25 * (cells[k - 1] + cells[k]) for k in range(1, N)]
    first, excess, excess_first = half[1], one, one
    for k in range(1, N - 1):
        g = 1.0 / (first + half[k + 1] + excess)
        n = first * g
        m = half[k + 1] * g
        emit(k, g, n, m)
        excess_first = excess_first + n * excess
        first = m * first
        excess = one + m * excess
    return first, excess_first, excess


def prepare_kernel(f_ref, c_ref, s_ref, rhs_ref, g_ref, n_ref, m_ref, mat_ref, ay_ref):
    def emit(k, g, n, m):
        g_ref[rows(k), :] = g
        n_ref[rows(k), :] = n
        m_ref[rows(k + 1), :] = m

    cells = [c_ref[rows(k), :] for k in range(N)]
    q, e0, e1 = eliminated(cells, emit)
    for k, part in enumerate((q, e0, e1)):
        mat_ref[rows(k), :] = part
    flux = None
    for y in range(N - 1):
        c0, c1 = c_ref[turned(y), :], c_ref[turned(y + 1), :]
        f0, f1 = f_ref[turned(y), :], f_ref[turned(y + 1), :]
        after = 0.5 * (c0 + c1) * (f1 - f0)
        ay_ref[turned(y), :] = after if flux is None else after - flux
        flux = after
    ay_ref[turned(N - 1), :] = -flux
    lane = lax.broadcasted_iota(jnp.int32, (N, LANES), 1)
    for k in range(N):
        c, f = cells[k], f_ref[rows(k), :]
        c_next = jnp.where(lane < LANES - 1, pltpu.roll(c, LANES - 1, 1), 0.0)
        f_next = jnp.where(lane < LANES - 1, pltpu.roll(f, LANES - 1, 1), 0.0)
        upper = 0.5 * (c + c_next) * (f_next - f)
        lower = jnp.where(lane > 0, pltpu.roll(upper, 1, 1), 0.5 * c * f)
        rhs_ref[rows(k), :] = 2.0 * f + s_ref[rows(k), :] + ay_ref[rows(k), :] + (upper - lower)


def x_forward_kernel(
    f_ref, c_ref, rhs_ref, g_ref, n_ref, m_ref, mat_ref, down_ref, up_ref, gr_ref, pay_ref, r_ref
):
    r_ref[...] = rhs_ref[...]
    flux_down = 0.5 * (down_ref[rows(1), :] + c_ref[turned(0), :]) * (
        f_ref[turned(0), :] - down_ref[rows(0), :]
    )
    flux_up = 0.5 * (up_ref[rows(1), :] + c_ref[turned(N - 1), :]) * (
        up_ref[rows(0), :] - f_ref[turned(N - 1), :]
    )
    r_ref[turned(0), :] = r_ref[turned(0), :] - flux_down
    r_ref[turned(N - 1), :] = r_ref[turned(N - 1), :] + flux_up
    r0, r1 = forward(lambda k: r_ref[rows(k), :], g_ref, n_ref, m_ref, gr_ref)
    values = [mat_ref[rows(k), :] for k in range(3)]
    values += [c_ref[rows(0), :], c_ref[rows(N - 1), :], r0, r1, jnp.zeros_like(r0)]
    for k, value in enumerate(values):
        pay_ref[pl.ds(k, N, stride=VALUES), :] = value
        pay_ref[pl.ds(N * VALUES + k, N, stride=VALUES), :] = value


def forward(right, g_ref, n_ref, m_ref, gr_ref):
    r0, carried = right(0), None
    for k in range(1, N):
        carried = right(k) if carried is None else right(k) + m_ref[rows(k), :] * carried
        if k < N - 1:
            r0 = r0 + n_ref[rows(k), :] * carried
            gr_ref[rows(k), :] = g_ref[rows(k), :] * carried
    return r0, carried


def backward(u0, u1, gr_ref, n_ref, m_ref, emit):
    emit(0, u0)
    emit(N - 1, u1)
    later = u1
    for k in range(N - 2, 0, -1):
        later = gr_ref[rows(k), :] + n_ref[rows(k), :] * u0 + m_ref[rows(k + 1), :] * later
        emit(k, later)


def coupled(in_ref, blocks):
    q, e0, e1, c0, c1, r0, r1 = (
        in_ref[pl.ds(k, blocks, stride=VALUES), :] for k in range(VALUES - 1)
    )
    block = lax.broadcasted_iota(jnp.int32, (blocks, LANES), 0)

    def before(value, s=1):
        return pltpu.roll(value, s, 0)

    def after(value, s=1):
        return pltpu.roll(value, blocks - s, 0)

    inside_low = block > 0
    inside_high = block < blocks - 1
    low = 0.25 * (jnp.where(inside_low, before(c1), 0.0) + c0)
    high = 0.25 * (jnp.where(inside_high, after(c0), 0.0) + c1)
    e0 = e0 + jnp.where(inside_low, 0.0, low)
    e1 = e1 + jnp.where(inside_high, 0.0, high)
    low = jnp.where(inside_low, low, 0.0)
    high = jnp.where(inside_high, high, 0.0)
    h = 1.0 / (q + high + e1)
    qh, eh, rh = q * h, e1 * h, r1 * h
    lower = low * before(qh)
    upper = qh * high
    excess = e0 + q * eh + low * before(eh)
    right = r0 + q * rh + low * before(rh)
    s = 1
    while s < blocks:
        g = 1.0 / (lower + upper + excess)
        lg, ug, eg, rg = lower * g, upper * g, excess * g, right * g
        excess = excess + lower * before(eg, s) + upper * after(eg, s)
        right = right + lower * before(rg, s) + upper * after(rg, s)
        lower, upper = lower * before(lg, s), upper * after(ug, s)
        s *= 2
    u0 = right / excess
    u1 = rh + qh * u0 + (high * h) * after(u0)
    return u0, u1


def x_middle_kernel(blocks, in_ref, out_ref):
    u0, u1 = coupled(in_ref, blocks)
    out_ref[...] = jnp.where(lax.axis_index("gx") < N, u0, u1)


def y_middle_kernel(blocks, in_ref, out_ref):
    u0, u1 = coupled(in_ref, blocks)
    out_ref[pl.ds(0, blocks, stride=2), :] = u0
    out_ref[pl.ds(1, blocks, stride=2), :] = u1


def matrix_kernel(c_ref, g_ref, n_ref, m_ref, mat_ref, low_ref, high_ref, last_ref):
    def emit(k, g, n, m):
        g_ref[rows(k), :] = g
        n_ref[rows(k), :] = n
        m_ref[rows(k + 1), :] = m

    cells = [c_ref[turned(k), :] for k in range(N)]
    q, e0, e1 = eliminated(cells, emit)
    for k, part in enumerate((q, e0, e1, cells[0], cells[N - 1])):
        mat_ref[rows(k), :] = part
    size = 64
    lane = lax.broadcasted_iota(jnp.int32, (size, LANES), 1)
    for start in range(0, N * N, size):
        c = c_ref[pl.ds(start, size), :]
        inner = jnp.where(lane < LANES - 1, 0.25 * (c + pltpu.roll(c, LANES - 1, 1)), 0.0)
        lower, upper = pltpu.roll(inner, 1, 1), inner
        excess = jnp.where((lane > 0) & (lane < LANES - 1), 1.0, 1.0 + 0.25 * c)
        for at, s in enumerate(ROUNDS):
            g = 1.0 / (lower + upper + excess)
            lg, ug, eg = lower * g, upper * g, excess * g
            low_ref[pl.ds(at * N * N + start, size), :] = lower * pltpu.roll(g, s, 1)
            high_ref[pl.ds(at * N * N + start, size), :] = upper * pltpu.roll(g, LANES - s, 1)
            excess = excess + lower * pltpu.roll(eg, s, 1) + upper * pltpu.roll(eg, LANES - s, 1)
            lower, upper = lower * pltpu.roll(lg, s, 1), upper * pltpu.roll(ug, LANES - s, 1)
        last_ref[pl.ds(start, size), :] = 1.0 / excess


def x_back_kernel(
    ret_ref, f_ref, gr_ref, n_ref, m_ref, gy_ref, ny_ref, my_ref, mat_ref, gry_ref, pay_ref, u_ref
):
    def emit(k, w):
        u_ref[rows(k), :] = w - 2.0 * f_ref[rows(k), :]

    backward(ret_ref[rows(0), :], ret_ref[rows(1), :], gr_ref, n_ref, m_ref, emit)
    r0, r1 = forward(lambda k: u_ref[turned(k), :], gy_ref, ny_ref, my_ref, gry_ref)
    values = [mat_ref[rows(k), :] for k in range(5)] + [r0, r1, jnp.zeros_like(r0)]
    for k, value in enumerate(values):
        pay_ref[pl.ds(k, N, stride=VALUES), :] = value


def y_back_kernel(
    ret_ref, f_ref, gry_ref, ny_ref, my_ref, low_ref, high_ref, last_ref, out_ref, u_ref
):
    def emit(k, u):
        u_ref[turned(k), :] = u

    backward(
        ret_ref[pl.ds(0, N, stride=2), :], ret_ref[pl.ds(1, N, stride=2), :], gry_ref, ny_ref, my_ref, emit
    )
    right = u_ref[...]
    for at, s in enumerate(ROUNDS):
        part = pl.ds(at * N * N, N * N)
        right = (
            right
            + low_ref[part, :] * pltpu.roll(right, s, 1)
            + high_ref[part, :] * pltpu.roll(right, LANES - s, 1)
        )
    out_ref[...] = f_ref[...] + right * last_ref[...]


def call(kernel, outs, scratch=(), flops=100_000):
    return pl.pallas_call(
        kernel,
        out_shape=outs,
        scratch_shapes=[pltpu.VMEM(dims, jnp.float32) for dims in scratch],
        compiler_params=pltpu.CompilerParams(vmem_limit_bytes=32 * 1024 * 1024),
    )


def body(field, conductance, source):
    size_x, size_y = lax.axis_size("gx"), lax.axis_size("gy")
    cells = N * N
    up = [(i, i + 1) for i in range(size_y - 1)]
    last = jnp.concatenate([field[:, N - 1], conductance[:, N - 1]])
    first = jnp.concatenate([field[:, 0], conductance[:, 0]])
    from_down = lax.ppermute(last, "gy", up)
    from_up = lax.ppermute(first, "gy", [(b, a) for a, b in up])
    f, c, s = (part.reshape(cells, LANES) for part in (field, conductance, source))
    whole = shape(cells, LANES)
    rhs, gx, nx, mx, mat_x = call(
        prepare_kernel, (whole, whole, whole, whole, shape(3 * N, LANES)), [(cells, LANES)]
    )(f, c, s)
    grx, pay = call(x_forward_kernel, (whole, shape(2 * N * VALUES, LANES)), [(cells, LANES)])(
        f, c, rhs, gx, nx, mx, mat_x, from_down, from_up
    )
    got = lax.all_to_all(pay.reshape(size_x, VALUES, LANES), "gx", 0, 0, tiled=True)
    gy, ny, my, mat_y, low, high, final = call(
        matrix_kernel,
        (whole, whole, whole, shape(5 * N, LANES))
        + (shape(len(ROUNDS) * cells, LANES), shape(len(ROUNDS) * cells, LANES), whole),
    )(c)
    solved = call(lambda *refs: x_middle_kernel(size_x, *refs), shape(size_x, LANES))(
        got.reshape(size_x * VALUES, LANES)
    )
    ret = lax.all_to_all(solved.reshape(size_x, 1, LANES), "gx", 0, 0, tiled=True)
    gry, pay = call(x_back_kernel, (whole, shape(N * VALUES, LANES)), [(cells, LANES)])(
        ret.reshape(size_x, LANES), f, grx, nx, mx, gy, ny, my, mat_y
    )
    got = lax.all_to_all(pay.reshape(size_y, VALUES, LANES), "gy", 0, 0, tiled=True)
    solved = call(lambda *refs: y_middle_kernel(size_y, *refs), shape(2 * size_y, LANES))(
        got.reshape(size_y * VALUES, LANES)
    )
    ret = lax.all_to_all(solved.reshape(size_y, 2, LANES), "gy", 0, 0, tiled=True)
    out = call(y_back_kernel, whole, [(cells, LANES)])(
        ret.reshape(2 * size_y, LANES), f, gry, ny, my, low, high, final
    )
    return out.reshape(field.shape)


def solution(mesh):
    spec = P("gx", "gy", None)
    return jax.shard_map(
        body, mesh=mesh, in_specs=(spec, spec, spec), out_specs=spec, check_vma=False
    )
```

```python
import jax
import jax.numpy as jnp
from jax import lax
from jax.experimental import pallas as pl
from jax.experimental.pallas import tpu as pltpu
from jax.sharding import PartitionSpec as P

N = 16
CELLS = N * N
LANES = 128
ROUNDS = (1, 2, 4, 8, 16, 32, 64)
RING_X = 4
CORES = 2


def rows(k):
    return pl.ds(N * k, N)


def turned(k):
    return pl.ds(k, N, stride=N)


def shape(*dims):
    return jax.ShapeDtypeStruct(dims, jnp.float32)


def eliminated(cells, g_ref, n_ref, m_ref):
    one = jnp.ones_like(cells[0])
    half = [None] + [0.25 * (cells[k - 1] + cells[k]) for k in range(1, N)]
    first, excess, excess_first = half[1], one, one
    for k in range(1, N - 1):
        g = 1.0 / (first + half[k + 1] + excess)
        n = first * g
        m = half[k + 1] * g
        g_ref[rows(k), :] = g
        n_ref[rows(k), :] = n
        m_ref[rows(k + 1), :] = m
        excess_first = excess_first + n * excess
        first = m * first
        excess = one + m * excess
    return first, excess_first, excess


def forward(right, g_ref, n_ref, m_ref, gr_ref):
    r0, carried = right(0), None
    for k in range(1, N):
        carried = right(k) if carried is None else right(k) + m_ref[rows(k), :] * carried
        if k < N - 1:
            r0 = r0 + n_ref[rows(k), :] * carried
            gr_ref[rows(k), :] = g_ref[rows(k), :] * carried
    return r0, carried


def backward(u0, u1, gr_ref, n_ref, m_ref, emit):
    emit(0, u0)
    emit(N - 1, u1)
    later = u1
    for k in range(N - 2, 0, -1):
        later = gr_ref[rows(k), :] + n_ref[rows(k), :] * u0 + m_ref[rows(k + 1), :] * later
        emit(k, later)


def join_blocks(left, right):
    ql, e0l, e1l, c0l, c1l, r0l, r1l = left
    qr, e0r, e1r, c0r, c1r, r0r, r1r = right
    face = 0.25 * (c1l + c0r)
    h = 1.0 / (ql + face + e1l)
    s, t = face * h, ql * h
    p = s * ql
    ew = e0r + s * e1l
    rw = r0r + s * r1l
    k = 1.0 / (qr + p + ew)
    qk, pk = qr * k, p * k
    joined = (
        qk * p, e0l + t * e1l + pk * ew, e1r + qk * ew, c0l, c1r, r0l + t * r1l + pk * rw, r1r + qk * rw
    )

    def expand(u0, u1):
        w = k * rw + qk * u1 + pk * u0
        return (u0, h * r1l + t * u0 + s * w), (w, u1)

    return joined, expand


def join_elements(left, right):
    kl, eal, ebl, ral, rbl = left
    kr, ear, ebr, rar, rbr = right
    em, rm = ebl + ear, rbl + rar
    k = 1.0 / (kl + kr + em)
    lk, rk = kl * k, kr * k
    joined = (lk * kr, eal + lk * em, ebr + rk * em, ral + lk * rm, rbr + rk * rm)

    def expand(u0, u1):
        middle = k * rm + lk * u0 + rk * u1
        return (u0, middle), (middle, u1)

    return joined, expand


def tree(parts, join):
    levels = []
    while len(parts) > 1:
        pairs = [join(parts[i], parts[i + 1]) for i in range(0, len(parts), 2)]
        levels.append([expand for _, expand in pairs])
        parts = [joined for joined, _ in pairs]

    def ends(u0, u1):
        found = [(u0, u1)]
        for expands in reversed(levels):
            found = [end for expand, both in zip(expands, found) for end in expand(*both)]
        return found

    return parts[0], ends


def chosen(found, scratch_ref, index):
    for i, (u0, u1) in enumerate(found):
        scratch_ref[rows(2 * i), :] = u0
        scratch_ref[rows(2 * i + 1), :] = u1
    return (
        scratch_ref[pl.ds(pl.multiple_of(index * 2 * N, 2 * N), N), :],
        scratch_ref[pl.ds(pl.multiple_of(index * 2 * N, 2 * N) + N, N), :],
    )


def parts_of(ref, i, count):
    return tuple(ref[rows(count * i + k), :] for k in range(count))


def replicate(pay_ref, values, copies):
    for i in range(copies):
        for k, value in enumerate(values):
            pay_ref[rows(len(values) * i + k), :] = value


def prepare_kernel(
    all_ref, f_ref, c_ref, last_ref, first_ref, rhs_ref, g_ref, n_ref, m_ref, mat_ref, ay_ref
):
    f_ref[...] = all_ref[pl.ds(0, CELLS), :]
    c_ref[...] = all_ref[pl.ds(CELLS, CELLS), :]
    for edge_ref, y in ((first_ref, 0), (last_ref, N - 1)):
        edge_ref[rows(0), :] = all_ref[turned(y), :]
        edge_ref[rows(1), :] = all_ref[pl.ds(CELLS + y, N, stride=N), :]
    cells = [all_ref[rows(N + k), :] for k in range(N)]
    for k, part in enumerate(eliminated(cells, g_ref, n_ref, m_ref)):
        mat_ref[rows(k), :] = part
    flux = None
    for y in range(N - 1):
        c0, c1 = c_ref[turned(y), :], c_ref[turned(y + 1), :]
        f0, f1 = f_ref[turned(y), :], f_ref[turned(y + 1), :]
        after = 0.5 * (c0 + c1) * (f1 - f0)
        ay_ref[turned(y), :] = after if flux is None else after - flux
        flux = after
    ay_ref[turned(N - 1), :] = -flux
    lane = lax.broadcasted_iota(jnp.int32, (N, LANES), 1)
    for k in range(N):
        c, f = cells[k], f_ref[rows(k), :]
        c_next = jnp.where(lane < LANES - 1, pltpu.roll(c, LANES - 1, 1), 0.0)
        f_next = jnp.where(lane < LANES - 1, pltpu.roll(f, LANES - 1, 1), 0.0)
        upper = 0.5 * (c + c_next) * (f_next - f)
        lower = jnp.where(lane > 0, pltpu.roll(upper, 1, 1), 0.5 * c * f)
        rhs_ref[rows(k), :] = 2.0 * f + all_ref[rows(2 * N + k), :] + ay_ref[rows(k), :] + (upper - lower)


def x_forward_kernel(
    f_ref, c_ref, rhs_ref, g_ref, n_ref, m_ref, mat_ref, maty_ref, down_ref, up_ref, gr_ref, pay_ref, elem_ref, r_ref
):
    r_ref[...] = rhs_ref[...]
    flux_down = 0.5 * (down_ref[rows(1), :] + c_ref[turned(0), :]) * (
        f_ref[turned(0), :] - down_ref[rows(0), :]
    )
    flux_up = 0.5 * (up_ref[rows(1), :] + c_ref[turned(N - 1), :]) * (
        up_ref[rows(0), :] - f_ref[turned(N - 1), :]
    )
    r_ref[turned(0), :] = r_ref[turned(0), :] - flux_down
    r_ref[turned(N - 1), :] = r_ref[turned(N - 1), :] + flux_up
    r0, r1 = forward(lambda k: r_ref[rows(k), :], g_ref, n_ref, m_ref, gr_ref)
    values = [mat_ref[rows(k), :] for k in range(3)]
    replicate(pay_ref, values + [c_ref[rows(0), :], c_ref[rows(N - 1), :], r0, r1], RING_X)
    q, e0, e1 = parts_of(maty_ref, 0, 3)
    face = 0.25 * (c_ref[turned(N - 1), :] + up_ref[rows(1), :])
    e0 = e0 + jnp.where(lax.axis_index("gy") == 0, 0.25 * c_ref[turned(0), :], 0.0)
    h = 1.0 / (q + face + e1)
    qh, fh = q * h, face * h
    replicate(elem_ref, (qh * face, e0 + qh * e1, fh * e1, qh, fh, h), 1)


def x_merge_kernel(rings, got_ref, pay_ref):
    whole, _ = tree([parts_of(got_ref, i, 7) for i in range(RING_X)], join_blocks)
    replicate(pay_ref, whole, rings)


def matrix_kernel(c_ref, g_ref, n_ref, m_ref, mat_ref, low_ref, high_ref, last_ref):
    cells = [c_ref[turned(k), :] for k in range(N)]
    for k, part in enumerate(eliminated(cells, g_ref, n_ref, m_ref)):
        mat_ref[rows(k), :] = part
    size = 64
    lane = lax.broadcasted_iota(jnp.int32, (size, LANES), 1)
    for start in range(0, CELLS, size):
        c = c_ref[pl.ds(start, size), :]
        inner = jnp.where(lane < LANES - 1, 0.25 * (c + pltpu.roll(c, LANES - 1, 1)), 0.0)
        lower, upper = pltpu.roll(inner, 1, 1), inner
        excess = jnp.where((lane > 0) & (lane < LANES - 1), 1.0, 1.0 + 0.25 * c)
        for at, s in enumerate(ROUNDS):
            g = 1.0 / (lower + upper + excess)
            lg, ug, eg = lower * g, upper * g, excess * g
            low_ref[pl.ds(at * CELLS + start, size), :] = lower * pltpu.roll(g, s, 1)
            high_ref[pl.ds(at * CELLS + start, size), :] = upper * pltpu.roll(g, LANES - s, 1)
            excess = excess + lower * pltpu.roll(eg, s, 1) + upper * pltpu.roll(eg, LANES - s, 1)
            lower, upper = lower * pltpu.roll(lg, s, 1), upper * pltpu.roll(ug, LANES - s, 1)
        last_ref[pl.ds(start, size), :] = 1.0 / excess


def x_back_kernel(
    rings, ring_ref, all_ref, f_ref, gr_ref, n_ref, m_ref, gy_ref, ny_ref, my_ref, mat_ref, gry_ref, pay_ref, hr_ref, u_ref, ends_ref
):
    me = lax.axis_index("gx")
    whole, ends = tree([parts_of(all_ref, i, 7) for i in range(rings)], join_blocks)
    q, e0, e1, c0, c1, r0, r1 = whole
    e0, e1 = e0 + 0.25 * c0, e1 + 0.25 * c1
    h = 1.0 / (q + e1)
    qh = q * h
    u0 = (r0 + qh * r1) / (e0 + qh * e1)
    u0, u1 = chosen(ends(u0, h * r1 + qh * u0), ends_ref, me // RING_X)
    _, ends = tree([parts_of(ring_ref, i, 7) for i in range(RING_X)], join_blocks)
    u0, u1 = chosen(ends(u0, u1), ends_ref, me % RING_X)

    def emit(k, w):
        u_ref[rows(k), :] = w - 2.0 * f_ref[rows(k), :]

    backward(u0, u1, gr_ref, n_ref, m_ref, emit)
    r0, r1 = forward(lambda k: u_ref[turned(k), :], gy_ref, ny_ref, my_ref, gry_ref)
    kappa, ea, eb, qh, fh, h = parts_of(mat_ref, 0, 6)
    replicate(pay_ref, (kappa, ea, eb, r0 + qh * r1, fh * r1), 1)
    hr_ref[...] = h * r1


def core_pair(own_ref, other_ref):
    odd = lax.axis_index("gy") % CORES == 1
    own, other = parts_of(own_ref, 0, 5), parts_of(other_ref, 0, 5)
    low = tuple(jnp.where(odd, b, a) for a, b in zip(own, other))
    high = tuple(jnp.where(odd, a, b) for a, b in zip(own, other))
    return join_elements(low, high)


def y_merge_kernel(rings, own_ref, other_ref, pay_ref):
    whole, _ = core_pair(own_ref, other_ref)
    replicate(pay_ref, whole, rings)


def y_back_kernel(
    rings, all_ref, own_ref, other_ref, mat_ref, hr_ref, f_ref, gry_ref, ny_ref, my_ref, low_ref, high_ref, last_ref, out_ref, u_ref, ends_ref
):
    me = lax.axis_index("gy")
    (kappa, ea, _, ra, _), ends = tree([parts_of(all_ref, i, 5) for i in range(rings)], join_elements)
    u0 = ra / (kappa + ea)
    u0, u1 = chosen(ends(u0, jnp.zeros_like(u0)), ends_ref, me // CORES)
    _, expand = core_pair(own_ref, other_ref)
    u0, u_next = chosen(expand(u0, u1), ends_ref, me % CORES)
    u1 = hr_ref[...] + mat_ref[rows(3), :] * u0 + mat_ref[rows(4), :] * u_next

    def emit(k, u):
        u_ref[turned(k), :] = u

    backward(u0, u1, gry_ref, ny_ref, my_ref, emit)
    right = u_ref[...]
    for at, s in enumerate(ROUNDS):
        part = pl.ds(at * CELLS, CELLS)
        right = (
            right
            + low_ref[part, :] * pltpu.roll(right, s, 1)
            + high_ref[part, :] * pltpu.roll(right, LANES - s, 1)
        )
    out_ref[...] = f_ref[...] + right * last_ref[...]


def call(kernel, outs, scratch=()):
    return pl.pallas_call(
        kernel,
        out_shape=outs,
        scratch_shapes=[pltpu.VMEM(part, jnp.float32) for part in scratch],
        compiler_params=pltpu.CompilerParams(vmem_limit_bytes=16 * 1024 * 1024),
    )


def gathered(pay, axis, groups):
    count = len(groups[0])
    got = lax.all_to_all(
        pay.reshape(count, -1, LANES), axis, 0, 0, tiled=True, axis_index_groups=groups
    )
    return got.reshape(-1, LANES)


def body(field, conductance, source):
    size_x, size_y = lax.axis_size("gx"), lax.axis_size("gy")
    rings_x, rings_y = size_x // RING_X, size_y // CORES
    f, c, s = (part.reshape(CELLS, LANES) for part in (field, conductance, source))
    whole, block = shape(CELLS, LANES), (CELLS, LANES)
    f, c, last, first, rhs, gx, nx, mx, mat_x = call(
        prepare_kernel,
        (whole, whole, shape(2 * N, LANES), shape(2 * N, LANES), whole, whole, whole, whole, shape(3 * N, LANES)),
        [block],
    )(jnp.concatenate([f, c, s]))
    up = [(i, i + 1) for i in range(size_y - 1)]
    from_down = lax.ppermute(last, "gy", up)
    from_up = lax.ppermute(first, "gy", [(b, a) for a, b in up])
    coefficients = shape(len(ROUNDS) * CELLS, LANES)
    gy, ny, my, mat_y, low, high, final = call(
        matrix_kernel, (whole, whole, whole, shape(3 * N, LANES), coefficients, coefficients, whole)
    )(c)
    grx, pay, mat_y = call(
        x_forward_kernel, (whole, shape(RING_X * 7 * N, LANES), shape(6 * N, LANES)), [block]
    )(f, c, rhs, gx, nx, mx, mat_x, mat_y, from_down, from_up)
    ring = gathered(pay, "gx", [[RING_X * i + j for j in range(RING_X)] for i in range(rings_x)])
    pay = call(lambda *refs: x_merge_kernel(rings_x, *refs), shape(rings_x * 7 * N, LANES))(ring)
    every = gathered(pay, "gx", [[RING_X * i + j for i in range(rings_x)] for j in range(RING_X)])
    gry, own, hr = call(
        lambda *refs: x_back_kernel(rings_x, *refs),
        (whole, shape(5 * N, LANES), shape(N, LANES)),
        [block, (2 * max(rings_x, RING_X) * N, LANES)],
    )(ring, every, f, grx, nx, mx, gy, ny, my, mat_y)
    other = lax.ppermute(own, "gy", [(i, i ^ 1) for i in range(size_y)])
    pay = call(lambda *refs: y_merge_kernel(rings_y, *refs), shape(rings_y * 5 * N, LANES))(own, other)
    every = gathered(pay, "gy", [[CORES * i + j for i in range(rings_y)] for j in range(CORES)])
    out = call(
        lambda *refs: y_back_kernel(rings_y, *refs), whole, [block, (2 * rings_y * N, LANES)]
    )(every, own, other, mat_y, hr, f, gry, ny, my, low, high, final)
    return out.reshape(field.shape)


def solution(mesh):
    spec = P("gx", "gy", None)
    return jax.shard_map(
        body, mesh=mesh, in_specs=(spec, spec, spec), out_specs=spec, check_vma=False
    )
```

```python
import jax
import jax.numpy as jnp
from jax import lax
from jax.experimental import pallas as pl
from jax.experimental.pallas import tpu as pltpu
from jax.sharding import PartitionSpec as P

N = 16
CELLS = N * N
LANES = 128
ROUNDS = (1, 2, 4, 8, 16, 32, 64)
NEAR_X = 8
NEAR_Y = 4


def rows(k):
    return pl.ds(N * k, N)


def turned(k):
    return pl.ds(k, N, stride=N)


def shape(*dims):
    return jax.ShapeDtypeStruct(dims, jnp.float32)


def eliminated(cells, g_ref, n_ref, m_ref):
    one = jnp.ones_like(cells[0])
    half = [None] + [0.25 * (cells[k - 1] + cells[k]) for k in range(1, N)]
    first, excess, excess_first = half[1], one, one
    for k in range(1, N - 1):
        g = 1.0 / (first + half[k + 1] + excess)
        n = first * g
        m = half[k + 1] * g
        g_ref[rows(k), :] = g
        n_ref[rows(k), :] = n
        m_ref[rows(k + 1), :] = m
        excess_first = excess_first + n * excess
        first = m * first
        excess = one + m * excess
    return first, excess_first, excess


def forward(right, g_ref, n_ref, m_ref, gr_ref):
    r0, carried = right(0), None
    for k in range(1, N):
        carried = right(k) if carried is None else right(k) + m_ref[rows(k), :] * carried
        if k < N - 1:
            r0 = r0 + n_ref[rows(k), :] * carried
            gr_ref[rows(k), :] = g_ref[rows(k), :] * carried
    return r0, carried


def backward(u0, u1, gr_ref, n_ref, m_ref, emit):
    emit(0, u0)
    emit(N - 1, u1)
    later = u1
    for k in range(N - 2, 0, -1):
        later = gr_ref[rows(k), :] + n_ref[rows(k), :] * u0 + m_ref[rows(k + 1), :] * later
        emit(k, later)


def join_blocks(left, right):
    ql, e0l, e1l, c0l, c1l, r0l, r1l = left
    qr, e0r, e1r, c0r, c1r, r0r, r1r = right
    face = 0.25 * (c1l + c0r)
    h = 1.0 / (ql + face + e1l)
    s, t = face * h, ql * h
    p = s * ql
    ew = e0r + s * e1l
    rw = r0r + s * r1l
    k = 1.0 / (qr + p + ew)
    qk, pk = qr * k, p * k
    joined = (
        qk * p, e0l + t * e1l + pk * ew, e1r + qk * ew, c0l, c1r, r0l + t * r1l + pk * rw, r1r + qk * rw
    )

    def expand(u0, u1):
        w = k * rw + qk * u1 + pk * u0
        return (u0, h * r1l + t * u0 + s * w), (w, u1)

    return joined, expand


def join_elements(left, right):
    kl, eal, ebl, ral, rbl = left
    kr, ear, ebr, rar, rbr = right
    em, rm = ebl + ear, rbl + rar
    k = 1.0 / (kl + kr + em)
    lk, rk = kl * k, kr * k
    joined = (lk * kr, eal + lk * em, ebr + rk * em, ral + lk * rm, rbr + rk * rm)

    def expand(u0, u1):
        middle = k * rm + lk * u0 + rk * u1
        return (u0, middle), (middle, u1)

    return joined, expand


def tree(parts, join):
    levels = []
    while len(parts) > 1:
        pairs = [join(parts[i], parts[i + 1]) for i in range(0, len(parts), 2)]
        levels.append([expand for _, expand in pairs])
        parts = [joined for joined, _ in pairs]

    def ends(u0, u1):
        found = [(u0, u1)]
        for expands in reversed(levels):
            found = [end for expand, both in zip(expands, found) for end in expand(*both)]
        return found

    return parts[0], ends


def chosen(found, scratch_ref, index):
    for i, (u0, u1) in enumerate(found):
        scratch_ref[rows(2 * i), :] = u0
        scratch_ref[rows(2 * i + 1), :] = u1
    return (
        scratch_ref[pl.ds(pl.multiple_of(index * 2 * N, 2 * N), N), :],
        scratch_ref[pl.ds(pl.multiple_of(index * 2 * N, 2 * N) + N, N), :],
    )


def parts_of(ref, i, count):
    return tuple(ref[rows(count * i + k), :] for k in range(count))


def replicate(pay_ref, values, copies):
    for i in range(copies):
        for k, value in enumerate(values):
            pay_ref[rows(len(values) * i + k), :] = value


def prepare_kernel(
    all_ref, f_ref, c_ref, last_ref, first_ref, rhs_ref, g_ref, n_ref, m_ref, mat_ref, ay_ref
):
    f_ref[...] = all_ref[pl.ds(0, CELLS), :]
    c_ref[...] = all_ref[pl.ds(CELLS, CELLS), :]
    for edge_ref, y in ((first_ref, 0), (last_ref, N - 1)):
        edge_ref[rows(0), :] = all_ref[turned(y), :]
        edge_ref[rows(1), :] = all_ref[pl.ds(CELLS + y, N, stride=N), :]
    cells = [all_ref[rows(N + k), :] for k in range(N)]
    for k, part in enumerate(eliminated(cells, g_ref, n_ref, m_ref)):
        mat_ref[rows(k), :] = part
    flux = None
    for y in range(N - 1):
        c0, c1 = c_ref[turned(y), :], c_ref[turned(y + 1), :]
        f0, f1 = f_ref[turned(y), :], f_ref[turned(y + 1), :]
        after = 0.5 * (c0 + c1) * (f1 - f0)
        ay_ref[turned(y), :] = after if flux is None else after - flux
        flux = after
    ay_ref[turned(N - 1), :] = -flux
    lane = lax.broadcasted_iota(jnp.int32, (N, LANES), 1)
    for k in range(N):
        c, f = cells[k], f_ref[rows(k), :]
        c_next = jnp.where(lane < LANES - 1, pltpu.roll(c, LANES - 1, 1), 0.0)
        f_next = jnp.where(lane < LANES - 1, pltpu.roll(f, LANES - 1, 1), 0.0)
        upper = 0.5 * (c + c_next) * (f_next - f)
        lower = jnp.where(lane > 0, pltpu.roll(upper, 1, 1), 0.5 * c * f)
        rhs_ref[rows(k), :] = 2.0 * f + all_ref[rows(2 * N + k), :] + ay_ref[rows(k), :] + (upper - lower)


def x_forward_kernel(
    f_ref, c_ref, rhs_ref, g_ref, n_ref, m_ref, mat_ref, maty_ref, down_ref, up_ref, gr_ref, pay_ref, elem_ref, r_ref
):
    r_ref[...] = rhs_ref[...]
    flux_down = 0.5 * (down_ref[rows(1), :] + c_ref[turned(0), :]) * (
        f_ref[turned(0), :] - down_ref[rows(0), :]
    )
    flux_up = 0.5 * (up_ref[rows(1), :] + c_ref[turned(N - 1), :]) * (
        up_ref[rows(0), :] - f_ref[turned(N - 1), :]
    )
    r_ref[turned(0), :] = r_ref[turned(0), :] - flux_down
    r_ref[turned(N - 1), :] = r_ref[turned(N - 1), :] + flux_up
    r0, r1 = forward(lambda k: r_ref[rows(k), :], g_ref, n_ref, m_ref, gr_ref)
    values = [mat_ref[rows(k), :] for k in range(3)]
    replicate(pay_ref, values + [c_ref[rows(0), :], c_ref[rows(N - 1), :], r0, r1], NEAR_X)
    q, e0, e1 = parts_of(maty_ref, 0, 3)
    face = 0.25 * (c_ref[turned(N - 1), :] + up_ref[rows(1), :])
    e0 = e0 + jnp.where(lax.axis_index("gy") == 0, 0.25 * c_ref[turned(0), :], 0.0)
    h = 1.0 / (q + face + e1)
    qh, fh = q * h, face * h
    replicate(elem_ref, (qh * face, e0 + qh * e1, fh * e1, qh, fh, h), 1)


def x_merge_kernel(far, got_ref, pay_ref):
    whole, _ = tree([parts_of(got_ref, i, 7) for i in range(NEAR_X)], join_blocks)
    replicate(pay_ref, whole, far)


def matrix_kernel(c_ref, g_ref, n_ref, m_ref, mat_ref, low_ref, high_ref, last_ref):
    cells = [c_ref[turned(k), :] for k in range(N)]
    for k, part in enumerate(eliminated(cells, g_ref, n_ref, m_ref)):
        mat_ref[rows(k), :] = part
    size = 64
    lane = lax.broadcasted_iota(jnp.int32, (size, LANES), 1)
    for start in range(0, CELLS, size):
        c = c_ref[pl.ds(start, size), :]
        inner = jnp.where(lane < LANES - 1, 0.25 * (c + pltpu.roll(c, LANES - 1, 1)), 0.0)
        lower, upper = pltpu.roll(inner, 1, 1), inner
        excess = jnp.where((lane > 0) & (lane < LANES - 1), 1.0, 1.0 + 0.25 * c)
        for at, s in enumerate(ROUNDS):
            g = 1.0 / (lower + upper + excess)
            lg, ug, eg = lower * g, upper * g, excess * g
            low_ref[pl.ds(at * CELLS + start, size), :] = lower * pltpu.roll(g, s, 1)
            high_ref[pl.ds(at * CELLS + start, size), :] = upper * pltpu.roll(g, LANES - s, 1)
            excess = excess + lower * pltpu.roll(eg, s, 1) + upper * pltpu.roll(eg, LANES - s, 1)
            lower, upper = lower * pltpu.roll(lg, s, 1), upper * pltpu.roll(ug, LANES - s, 1)
        last_ref[pl.ds(start, size), :] = 1.0 / excess


def x_back_kernel(
    far, near_ref, all_ref, f_ref, gr_ref, n_ref, m_ref, gy_ref, ny_ref, my_ref, mat_ref, gry_ref, pay_ref, hr_ref, u_ref, ends_ref
):
    me = lax.axis_index("gx")
    whole, ends = tree([parts_of(all_ref, i, 7) for i in range(far)], join_blocks)
    q, e0, e1, c0, c1, r0, r1 = whole
    e0, e1 = e0 + 0.25 * c0, e1 + 0.25 * c1
    h = 1.0 / (q + e1)
    qh = q * h
    u0 = (r0 + qh * r1) / (e0 + qh * e1)
    u0, u1 = chosen(ends(u0, h * r1 + qh * u0), ends_ref, me // NEAR_X)
    _, ends = tree([parts_of(near_ref, i, 7) for i in range(NEAR_X)], join_blocks)
    u0, u1 = chosen(ends(u0, u1), ends_ref, me % NEAR_X)

    def emit(k, w):
        u_ref[rows(k), :] = w - 2.0 * f_ref[rows(k), :]

    backward(u0, u1, gr_ref, n_ref, m_ref, emit)
    r0, r1 = forward(lambda k: u_ref[turned(k), :], gy_ref, ny_ref, my_ref, gry_ref)
    kappa, ea, eb, qh, fh, h = parts_of(mat_ref, 0, 6)
    replicate(pay_ref, (kappa, ea, eb, r0 + qh * r1, fh * r1), NEAR_Y)
    hr_ref[...] = h * r1


def y_merge_kernel(far, got_ref, pay_ref):
    whole, _ = tree([parts_of(got_ref, i, 5) for i in range(NEAR_Y)], join_elements)
    replicate(pay_ref, whole, far)


def y_back_kernel(
    far, near_ref, all_ref, mat_ref, hr_ref, f_ref, gry_ref, ny_ref, my_ref, low_ref, high_ref, last_ref, out_ref, u_ref, ends_ref
):
    me = lax.axis_index("gy")
    (kappa, ea, _, ra, _), ends = tree([parts_of(all_ref, i, 5) for i in range(far)], join_elements)
    u0 = ra / (kappa + ea)
    u0, u1 = chosen(ends(u0, jnp.zeros_like(u0)), ends_ref, me // NEAR_Y)
    _, ends = tree([parts_of(near_ref, i, 5) for i in range(NEAR_Y)], join_elements)
    u0, u_next = chosen(ends(u0, u1), ends_ref, me % NEAR_Y)
    u1 = hr_ref[...] + mat_ref[rows(3), :] * u0 + mat_ref[rows(4), :] * u_next

    def emit(k, u):
        u_ref[turned(k), :] = u

    backward(u0, u1, gry_ref, ny_ref, my_ref, emit)
    right = u_ref[...]
    for at, s in enumerate(ROUNDS):
        part = pl.ds(at * CELLS, CELLS)
        right = (
            right
            + low_ref[part, :] * pltpu.roll(right, s, 1)
            + high_ref[part, :] * pltpu.roll(right, LANES - s, 1)
        )
    out_ref[...] = f_ref[...] + right * last_ref[...]


def call(kernel, outs, scratch=()):
    return pl.pallas_call(
        kernel,
        out_shape=outs,
        scratch_shapes=[pltpu.VMEM(part, jnp.float32) for part in scratch],
        compiler_params=pltpu.CompilerParams(vmem_limit_bytes=16 * 1024 * 1024),
    )


def gathered(pay, axis, groups):
    count = len(groups[0])
    got = lax.all_to_all(
        pay.reshape(count, -1, LANES), axis, 0, 0, tiled=True, axis_index_groups=groups
    )
    return got.reshape(-1, LANES)


def body(field, conductance, source):
    size_x, size_y = lax.axis_size("gx"), lax.axis_size("gy")
    far_x, far_y = size_x // NEAR_X, size_y // NEAR_Y
    f, c, s = (part.reshape(CELLS, LANES) for part in (field, conductance, source))
    whole, block = shape(CELLS, LANES), (CELLS, LANES)
    f, c, last, first, rhs, gx, nx, mx, mat_x = call(
        prepare_kernel,
        (whole, whole, shape(2 * N, LANES), shape(2 * N, LANES), whole, whole, whole, whole, shape(3 * N, LANES)),
        [block],
    )(jnp.concatenate([f, c, s]))
    up = [(i, i + 1) for i in range(size_y - 1)]
    from_down = lax.ppermute(last, "gy", up)
    from_up = lax.ppermute(first, "gy", [(b, a) for a, b in up])
    coefficients = shape(len(ROUNDS) * CELLS, LANES)
    gy, ny, my, mat_y, low, high, final = call(
        matrix_kernel, (whole, whole, whole, shape(3 * N, LANES), coefficients, coefficients, whole)
    )(c)
    grx, pay, mat_y = call(
        x_forward_kernel, (whole, shape(NEAR_X * 7 * N, LANES), shape(6 * N, LANES)), [block]
    )(f, c, rhs, gx, nx, mx, mat_x, mat_y, from_down, from_up)
    near = gathered(pay, "gx", [[NEAR_X * i + j for j in range(NEAR_X)] for i in range(far_x)])
    pay = call(lambda *refs: x_merge_kernel(far_x, *refs), shape(far_x * 7 * N, LANES))(near)
    every = gathered(pay, "gx", [[NEAR_X * i + j for i in range(far_x)] for j in range(NEAR_X)])
    gry, pay, hr = call(
        lambda *refs: x_back_kernel(far_x, *refs),
        (whole, shape(NEAR_Y * 5 * N, LANES), shape(N, LANES)),
        [block, (2 * max(far_x, NEAR_X) * N, LANES)],
    )(near, every, f, grx, nx, mx, gy, ny, my, mat_y)
    near = gathered(pay, "gy", [[NEAR_Y * i + j for j in range(NEAR_Y)] for i in range(far_y)])
    pay = call(lambda *refs: y_merge_kernel(far_y, *refs), shape(far_y * 5 * N, LANES))(near)
    every = gathered(pay, "gy", [[NEAR_Y * i + j for i in range(far_y)] for j in range(NEAR_Y)])
    out = call(
        lambda *refs: y_back_kernel(far_y, *refs), whole, [block, (2 * max(far_y, NEAR_Y) * N, LANES)]
    )(near, every, mat_y, hr, f, gry, ny, my, low, high, final)
    return out.reshape(field.shape)


def solution(mesh):
    spec = P("gx", "gy", None)
    return jax.shard_map(
        body, mesh=mesh, in_specs=(spec, spec, spec), out_specs=spec, check_vma=False
    )
```

```python
import jax
import jax.numpy as jnp
from jax import lax
from jax.experimental import pallas as pl
from jax.experimental.pallas import tpu as pltpu
from jax.sharding import PartitionSpec as P

N = 16
CELLS = N * N
LANES = 128
ROUNDS = (1, 2, 4, 8, 16, 32, 64)
NEAR_X = 8
NEAR_Y = 4


def rows(k):
    return pl.ds(N * k, N)


def turned(k):
    return pl.ds(k, N, stride=N)


def shape(*dims):
    return jax.ShapeDtypeStruct(dims, jnp.float32)


def eliminated(cells, g_ref, n_ref, m_ref):
    one = jnp.ones_like(cells[0])
    half = [None] + [0.25 * (cells[k - 1] + cells[k]) for k in range(1, N)]
    first, excess, excess_first = half[1], one, one
    for k in range(1, N - 1):
        g = 1.0 / (first + half[k + 1] + excess)
        n = first * g
        m = half[k + 1] * g
        g_ref[rows(k), :] = g
        n_ref[rows(k), :] = n
        m_ref[rows(k + 1), :] = m
        excess_first = excess_first + n * excess
        first = m * first
        excess = one + m * excess
    return first, excess_first, excess


def forward(right, g_ref, n_ref, m_ref, gr_ref):
    r0, carried = right(0), None
    for k in range(1, N):
        carried = right(k) if carried is None else right(k) + m_ref[rows(k), :] * carried
        if k < N - 1:
            r0 = r0 + n_ref[rows(k), :] * carried
            gr_ref[rows(k), :] = g_ref[rows(k), :] * carried
    return r0, carried


def backward(u0, u1, gr_ref, n_ref, m_ref, emit):
    emit(0, u0)
    emit(N - 1, u1)
    later = u1
    for k in range(N - 2, 0, -1):
        later = gr_ref[rows(k), :] + n_ref[rows(k), :] * u0 + m_ref[rows(k + 1), :] * later
        emit(k, later)


def join_blocks(left, right):
    ql, e0l, e1l, c0l, c1l, r0l, r1l = left
    qr, e0r, e1r, c0r, c1r, r0r, r1r = right
    face = 0.25 * (c1l + c0r)
    h = 1.0 / (ql + face + e1l)
    s, t = face * h, ql * h
    p = s * ql
    ew = e0r + s * e1l
    rw = r0r + s * r1l
    k = 1.0 / (qr + p + ew)
    qk, pk = qr * k, p * k
    joined = (
        qk * p, e0l + t * e1l + pk * ew, e1r + qk * ew, c0l, c1r, r0l + t * r1l + pk * rw, r1r + qk * rw
    )

    def expand(u0, u1):
        w = k * rw + qk * u1 + pk * u0
        return (u0, h * r1l + t * u0 + s * w), (w, u1)

    return joined, expand


def join_elements(left, right):
    kl, eal, ebl, ral, rbl = left
    kr, ear, ebr, rar, rbr = right
    em, rm = ebl + ear, rbl + rar
    k = 1.0 / (kl + kr + em)
    lk, rk = kl * k, kr * k
    joined = (lk * kr, eal + lk * em, ebr + rk * em, ral + lk * rm, rbr + rk * rm)

    def expand(u0, u1):
        middle = k * rm + lk * u0 + rk * u1
        return (u0, middle), (middle, u1)

    return joined, expand


def tree(parts, join):
    levels = []
    while len(parts) > 1:
        pairs = [join(parts[i], parts[i + 1]) for i in range(0, len(parts), 2)]
        levels.append([expand for _, expand in pairs])
        parts = [joined for joined, _ in pairs]

    def ends(u0, u1):
        found = [(u0, u1)]
        for expands in reversed(levels):
            found = [end for expand, both in zip(expands, found) for end in expand(*both)]
        return found

    return parts[0], ends


def chosen(found, scratch_ref, index):
    for i, (u0, u1) in enumerate(found):
        scratch_ref[rows(2 * i), :] = u0
        scratch_ref[rows(2 * i + 1), :] = u1
    return (
        scratch_ref[pl.ds(pl.multiple_of(index * 2 * N, 2 * N), N), :],
        scratch_ref[pl.ds(pl.multiple_of(index * 2 * N, 2 * N) + N, N), :],
    )


def parts_of(ref, i, count):
    return tuple(ref[rows(count * i + k), :] for k in range(count))


def replicate(pay_ref, values, copies):
    for i in range(copies):
        for k, value in enumerate(values):
            pay_ref[rows(len(values) * i + k), :] = value


def prepare_kernel(
    all_ref, f_ref, c_ref, outer_ref, inner_ref, rhs_ref, g_ref, n_ref, m_ref, mat_ref, ay_ref
):
    odd = lax.axis_index("gy") % 2
    f_ref[...] = all_ref[pl.ds(0, CELLS), :]
    c_ref[...] = all_ref[pl.ds(CELLS, CELLS), :]
    for at in (0, 1):
        first, last = (all_ref[pl.ds(CELLS * at + y, N, stride=N), :] for y in (0, N - 1))
        outer_ref[rows(at), :] = jnp.where(odd == 1, last, first)
        inner_ref[rows(at), :] = jnp.where(odd == 1, first, last)
    cells = [all_ref[rows(N + k), :] for k in range(N)]
    for k, part in enumerate(eliminated(cells, g_ref, n_ref, m_ref)):
        mat_ref[rows(k), :] = part
    flux = None
    for y in range(N - 1):
        c0, c1 = c_ref[turned(y), :], c_ref[turned(y + 1), :]
        f0, f1 = f_ref[turned(y), :], f_ref[turned(y + 1), :]
        after = 0.5 * (c0 + c1) * (f1 - f0)
        ay_ref[turned(y), :] = after if flux is None else after - flux
        flux = after
    ay_ref[turned(N - 1), :] = -flux
    lane = lax.broadcasted_iota(jnp.int32, (N, LANES), 1)
    for k in range(N):
        c, f = cells[k], f_ref[rows(k), :]
        c_next = jnp.where(lane < LANES - 1, pltpu.roll(c, LANES - 1, 1), 0.0)
        f_next = jnp.where(lane < LANES - 1, pltpu.roll(f, LANES - 1, 1), 0.0)
        upper = 0.5 * (c + c_next) * (f_next - f)
        lower = jnp.where(lane > 0, pltpu.roll(upper, 1, 1), 0.5 * c * f)
        rhs_ref[rows(k), :] = 2.0 * f + all_ref[rows(2 * N + k), :] + ay_ref[rows(k), :] + (upper - lower)


def x_forward_kernel(
    f_ref, c_ref, rhs_ref, g_ref, n_ref, m_ref, mat_ref, maty_ref, outer_ref, inner_ref, gr_ref, pay_ref, elem_ref, r_ref, down_ref, up_ref
):
    odd = lax.axis_index("gy") % 2 == 1
    down_ref[...] = jnp.where(odd, inner_ref[...], outer_ref[...])
    up_ref[...] = jnp.where(odd, outer_ref[...], inner_ref[...])
    r_ref[...] = rhs_ref[...]
    flux_down = 0.5 * (down_ref[rows(1), :] + c_ref[turned(0), :]) * (
        f_ref[turned(0), :] - down_ref[rows(0), :]
    )
    flux_up = 0.5 * (up_ref[rows(1), :] + c_ref[turned(N - 1), :]) * (
        up_ref[rows(0), :] - f_ref[turned(N - 1), :]
    )
    r_ref[turned(0), :] = r_ref[turned(0), :] - flux_down
    r_ref[turned(N - 1), :] = r_ref[turned(N - 1), :] + flux_up
    r0, r1 = forward(lambda k: r_ref[rows(k), :], g_ref, n_ref, m_ref, gr_ref)
    values = [mat_ref[rows(k), :] for k in range(3)]
    replicate(pay_ref, values + [c_ref[rows(0), :], c_ref[rows(N - 1), :], r0, r1], NEAR_X)
    q, e0, e1 = parts_of(maty_ref, 0, 3)
    face = 0.25 * (c_ref[turned(N - 1), :] + up_ref[rows(1), :])
    e0 = e0 + jnp.where(lax.axis_index("gy") == 0, 0.25 * c_ref[turned(0), :], 0.0)
    h = 1.0 / (q + face + e1)
    qh, fh = q * h, face * h
    replicate(elem_ref, (qh * face, e0 + qh * e1, fh * e1, qh, fh, h), 1)


def x_merge_kernel(far, got_ref, pay_ref):
    whole, _ = tree([parts_of(got_ref, i, 7) for i in range(NEAR_X)], join_blocks)
    replicate(pay_ref, whole, far)


def matrix_kernel(c_ref, g_ref, n_ref, m_ref, mat_ref, low_ref, high_ref, last_ref):
    cells = [c_ref[turned(k), :] for k in range(N)]
    for k, part in enumerate(eliminated(cells, g_ref, n_ref, m_ref)):
        mat_ref[rows(k), :] = part
    size = 256
    lane = lax.broadcasted_iota(jnp.int32, (size, LANES), 1)
    for start in range(0, CELLS, size):
        c = c_ref[pl.ds(start, size), :]
        inner = jnp.where(lane < LANES - 1, 0.25 * (c + pltpu.roll(c, LANES - 1, 1)), 0.0)
        lower, upper = pltpu.roll(inner, 1, 1), inner
        excess = jnp.where((lane > 0) & (lane < LANES - 1), 1.0, 1.0 + 0.25 * c)
        for at, s in enumerate(ROUNDS):
            g = 1.0 / (lower + upper + excess)
            lg, ug, eg = lower * g, upper * g, excess * g
            low_ref[pl.ds(at * CELLS + start, size), :] = lower * pltpu.roll(g, s, 1)
            high_ref[pl.ds(at * CELLS + start, size), :] = upper * pltpu.roll(g, LANES - s, 1)
            excess = excess + lower * pltpu.roll(eg, s, 1) + upper * pltpu.roll(eg, LANES - s, 1)
            lower, upper = lower * pltpu.roll(lg, s, 1), upper * pltpu.roll(ug, LANES - s, 1)
        last_ref[pl.ds(start, size), :] = 1.0 / excess


def x_back_kernel(
    far, near_ref, all_ref, f_ref, gr_ref, n_ref, m_ref, gy_ref, ny_ref, my_ref, mat_ref, gry_ref, pay_ref, hr_ref, u_ref, ends_ref
):
    me = lax.axis_index("gx")
    whole, ends = tree([parts_of(all_ref, i, 7) for i in range(far)], join_blocks)
    q, e0, e1, c0, c1, r0, r1 = whole
    e0, e1 = e0 + 0.25 * c0, e1 + 0.25 * c1
    h = 1.0 / (q + e1)
    qh = q * h
    u0 = (r0 + qh * r1) / (e0 + qh * e1)
    u0, u1 = chosen(ends(u0, h * r1 + qh * u0), ends_ref, me // NEAR_X)
    _, ends = tree([parts_of(near_ref, i, 7) for i in range(NEAR_X)], join_blocks)
    u0, u1 = chosen(ends(u0, u1), ends_ref, me % NEAR_X)

    def emit(k, w):
        u_ref[rows(k), :] = w - 2.0 * f_ref[rows(k), :]

    backward(u0, u1, gr_ref, n_ref, m_ref, emit)
    r0, r1 = forward(lambda k: u_ref[turned(k), :], gy_ref, ny_ref, my_ref, gry_ref)
    kappa, ea, eb, qh, fh, h = parts_of(mat_ref, 0, 6)
    replicate(pay_ref, (kappa, ea, eb, r0 + qh * r1, fh * r1), NEAR_Y)
    hr_ref[...] = h * r1


def y_merge_kernel(far, got_ref, pay_ref):
    whole, _ = tree([parts_of(got_ref, i, 5) for i in range(NEAR_Y)], join_elements)
    replicate(pay_ref, whole, far)


def y_back_kernel(
    far, near_ref, all_ref, mat_ref, hr_ref, f_ref, gry_ref, ny_ref, my_ref, low_ref, high_ref, last_ref, out_ref, u_ref, ends_ref
):
    me = lax.axis_index("gy")
    (kappa, ea, _, ra, _), ends = tree([parts_of(all_ref, i, 5) for i in range(far)], join_elements)
    u0 = ra / (kappa + ea)
    u0, u1 = chosen(ends(u0, jnp.zeros_like(u0)), ends_ref, me // NEAR_Y)
    _, ends = tree([parts_of(near_ref, i, 5) for i in range(NEAR_Y)], join_elements)
    u0, u_next = chosen(ends(u0, u1), ends_ref, me % NEAR_Y)
    u1 = hr_ref[...] + mat_ref[rows(3), :] * u0 + mat_ref[rows(4), :] * u_next

    def emit(k, u):
        u_ref[turned(k), :] = u

    backward(u0, u1, gry_ref, ny_ref, my_ref, emit)
    right = u_ref[...]
    for at, s in enumerate(ROUNDS):
        part = pl.ds(at * CELLS, CELLS)
        right = (
            right
            + low_ref[part, :] * pltpu.roll(right, s, 1)
            + high_ref[part, :] * pltpu.roll(right, LANES - s, 1)
        )
    out_ref[...] = f_ref[...] + right * last_ref[...]


def call(kernel, outs, scratch=()):
    return pl.pallas_call(
        kernel,
        out_shape=outs,
        scratch_shapes=[pltpu.VMEM(part, jnp.float32) for part in scratch],
        compiler_params=pltpu.CompilerParams(vmem_limit_bytes=16 * 1024 * 1024),
    )


def gathered(pay, axis, groups):
    count = len(groups[0])
    got = lax.all_to_all(
        pay.reshape(count, -1, LANES), axis, 0, 0, tiled=True, axis_index_groups=groups
    )
    return got.reshape(-1, LANES)


def body(field, conductance, source):
    size_x, size_y = lax.axis_size("gx"), lax.axis_size("gy")
    far_x, far_y = size_x // NEAR_X, size_y // NEAR_Y
    f, c, s = (part.reshape(CELLS, LANES) for part in (field, conductance, source))
    whole, block = shape(CELLS, LANES), (CELLS, LANES)
    f, c, outer, inner, rhs, gx, nx, mx, mat_x = call(
        prepare_kernel,
        (whole, whole, shape(2 * N, LANES), shape(2 * N, LANES), whole, whole, whole, whole, shape(3 * N, LANES)),
        [block],
    )(jnp.concatenate([f, c, s]))
    across = [(i, i + 1) for i in range(1, size_y - 1, 2)]
    across += [(b, a) for a, b in across]
    outer = lax.ppermute(outer, "gy", across)
    inner = lax.ppermute(inner, "gy", [(i, i ^ 1) for i in range(size_y)])
    coefficients = shape(len(ROUNDS) * CELLS, LANES)
    gy, ny, my, mat_y, low, high, final = call(
        matrix_kernel, (whole, whole, whole, shape(3 * N, LANES), coefficients, coefficients, whole)
    )(c)
    grx, pay, mat_y = call(
        x_forward_kernel, (whole, shape(NEAR_X * 7 * N, LANES), shape(6 * N, LANES)), [block, (2 * N, LANES), (2 * N, LANES)]
    )(f, c, rhs, gx, nx, mx, mat_x, mat_y, outer, inner)
    near = gathered(pay, "gx", [[NEAR_X * i + j for j in range(NEAR_X)] for i in range(far_x)])
    pay = call(lambda *refs: x_merge_kernel(far_x, *refs), shape(far_x * 7 * N, LANES))(near)
    every = gathered(pay, "gx", [[NEAR_X * i + j for i in range(far_x)] for j in range(NEAR_X)])
    gry, pay, hr = call(
        lambda *refs: x_back_kernel(far_x, *refs),
        (whole, shape(NEAR_Y * 5 * N, LANES), shape(N, LANES)),
        [block, (2 * max(far_x, NEAR_X) * N, LANES)],
    )(near, every, f, grx, nx, mx, gy, ny, my, mat_y)
    near = gathered(pay, "gy", [[NEAR_Y * i + j for j in range(NEAR_Y)] for i in range(far_y)])
    pay = call(lambda *refs: y_merge_kernel(far_y, *refs), shape(far_y * 5 * N, LANES))(near)
    every = gathered(pay, "gy", [[NEAR_Y * i + j for i in range(far_y)] for j in range(NEAR_Y)])
    out = call(
        lambda *refs: y_back_kernel(far_y, *refs), whole, [block, (2 * max(far_y, NEAR_Y) * N, LANES)]
    )(near, every, mat_y, hr, f, gry, ny, my, low, high, final)
    return out.reshape(field.shape)


def solution(mesh):
    spec = P("gx", "gy", None)
    return jax.shard_map(
        body, mesh=mesh, in_specs=(spec, spec, spec), out_specs=spec, check_vma=False
    )
```

```python
import jax
import jax.numpy as jnp
from jax import lax
from jax.experimental import pallas as pl
from jax.experimental.pallas import tpu as pltpu
from jax.sharding import PartitionSpec as P

N = 16
CELLS = N * N
LANES = 128
SEGMENTS = LANES // N
ROUNDS = (1, 2, 4)
NEAR_X = 8
NEAR_Y = 4


def rows(k):
    return pl.ds(N * k, N)


def turned(k):
    return pl.ds(k, N, stride=N)


def shape(*dims):
    return jax.ShapeDtypeStruct(dims, jnp.float32)


def eliminated(cells, g_ref, n_ref, m_ref):
    one = jnp.ones_like(cells[0])
    half = [None] + [0.25 * (cells[k - 1] + cells[k]) for k in range(1, N)]
    first, excess, excess_first = half[1], one, one
    for k in range(1, N - 1):
        g = 1.0 / (first + half[k + 1] + excess)
        n = first * g
        m = half[k + 1] * g
        g_ref[rows(k), :] = g
        n_ref[rows(k), :] = n
        m_ref[rows(k + 1), :] = m
        excess_first = excess_first + n * excess
        first = m * first
        excess = one + m * excess
    return first, excess_first, excess


def forward(right, g_ref, n_ref, m_ref, gr_ref):
    r0, carried = right(0), None
    for k in range(1, N):
        carried = right(k) if carried is None else right(k) + m_ref[rows(k), :] * carried
        if k < N - 1:
            r0 = r0 + n_ref[rows(k), :] * carried
            gr_ref[rows(k), :] = g_ref[rows(k), :] * carried
    return r0, carried


def backward(u0, u1, gr_ref, n_ref, m_ref, emit):
    emit(0, u0)
    emit(N - 1, u1)
    later = u1
    for k in range(N - 2, 0, -1):
        later = gr_ref[rows(k), :] + n_ref[rows(k), :] * u0 + m_ref[rows(k + 1), :] * later
        emit(k, later)


def join_blocks(left, right):
    ql, e0l, e1l, c0l, c1l, r0l, r1l = left
    qr, e0r, e1r, c0r, c1r, r0r, r1r = right
    face = 0.25 * (c1l + c0r)
    h = 1.0 / (ql + face + e1l)
    s, t = face * h, ql * h
    p = s * ql
    ew = e0r + s * e1l
    rw = r0r + s * r1l
    k = 1.0 / (qr + p + ew)
    qk, pk = qr * k, p * k
    joined = (
        qk * p, e0l + t * e1l + pk * ew, e1r + qk * ew, c0l, c1r, r0l + t * r1l + pk * rw, r1r + qk * rw
    )

    def expand(u0, u1):
        w = k * rw + qk * u1 + pk * u0
        return (u0, h * r1l + t * u0 + s * w), (w, u1)

    return joined, expand


def join_elements(left, right):
    kl, eal, ebl, ral, rbl = left
    kr, ear, ebr, rar, rbr = right
    em, rm = ebl + ear, rbl + rar
    k = 1.0 / (kl + kr + em)
    lk, rk = kl * k, kr * k
    joined = (lk * kr, eal + lk * em, ebr + rk * em, ral + lk * rm, rbr + rk * rm)

    def expand(u0, u1):
        middle = k * rm + lk * u0 + rk * u1
        return (u0, middle), (middle, u1)

    return joined, expand


def tree(parts, join):
    levels = []
    while len(parts) > 1:
        pairs = [join(parts[i], parts[i + 1]) for i in range(0, len(parts), 2)]
        levels.append([expand for _, expand in pairs])
        parts = [joined for joined, _ in pairs]

    def ends(u0, u1):
        found = [(u0, u1)]
        for expands in reversed(levels):
            found = [end for expand, both in zip(expands, found) for end in expand(*both)]
        return found

    return parts[0], ends


def chosen(found, scratch_ref, index):
    for i, (u0, u1) in enumerate(found):
        scratch_ref[rows(2 * i), :] = u0
        scratch_ref[rows(2 * i + 1), :] = u1
    return (
        scratch_ref[pl.ds(pl.multiple_of(index * 2 * N, 2 * N), N), :],
        scratch_ref[pl.ds(pl.multiple_of(index * 2 * N, 2 * N) + N, N), :],
    )


def parts_of(ref, i, count):
    return tuple(ref[rows(count * i + k), :] for k in range(count))


def replicate(pay_ref, values, copies):
    for i in range(copies):
        for k, value in enumerate(values):
            pay_ref[rows(len(values) * i + k), :] = value


def edges_kernel(all_ref, outer_ref, inner_ref):
    odd = lax.axis_index("gy") % 2 == 1
    for at in (0, 1):
        first, last = (all_ref[pl.ds(CELLS * at + y, N, stride=N), :] for y in (0, N - 1))
        outer_ref[rows(at), :] = jnp.where(odd, last, first)
        inner_ref[rows(at), :] = jnp.where(odd, first, last)


def prepare_kernel(all_ref, f_ref, c_ref, rhs_ref, g_ref, n_ref, m_ref, mat_ref, ay_ref):
    f_ref[...] = all_ref[pl.ds(0, CELLS), :]
    c_ref[...] = all_ref[pl.ds(CELLS, CELLS), :]
    cells = [all_ref[rows(N + k), :] for k in range(N)]
    for k, part in enumerate(eliminated(cells, g_ref, n_ref, m_ref)):
        mat_ref[rows(k), :] = part
    flux = None
    for y in range(N - 1):
        c0, c1 = c_ref[turned(y), :], c_ref[turned(y + 1), :]
        f0, f1 = f_ref[turned(y), :], f_ref[turned(y + 1), :]
        after = 0.5 * (c0 + c1) * (f1 - f0)
        ay_ref[turned(y), :] = after if flux is None else after - flux
        flux = after
    ay_ref[turned(N - 1), :] = -flux
    lane = lax.broadcasted_iota(jnp.int32, (N, LANES), 1)
    for k in range(N):
        c, f = cells[k], f_ref[rows(k), :]
        c_next = jnp.where(lane < LANES - 1, pltpu.roll(c, LANES - 1, 1), 0.0)
        f_next = jnp.where(lane < LANES - 1, pltpu.roll(f, LANES - 1, 1), 0.0)
        upper = 0.5 * (c + c_next) * (f_next - f)
        lower = jnp.where(lane > 0, pltpu.roll(upper, 1, 1), 0.5 * c * f)
        rhs_ref[rows(k), :] = 2.0 * f + all_ref[rows(2 * N + k), :] + ay_ref[rows(k), :] + (upper - lower)


def x_forward_kernel(
    f_ref, c_ref, rhs_ref, g_ref, n_ref, m_ref, mat_ref, maty_ref, outer_ref, inner_ref, gr_ref, pay_ref, elem_ref, r_ref, down_ref, up_ref
):
    odd = lax.axis_index("gy") % 2 == 1
    down_ref[...] = jnp.where(odd, inner_ref[...], outer_ref[...])
    up_ref[...] = jnp.where(odd, outer_ref[...], inner_ref[...])
    r_ref[...] = rhs_ref[...]
    flux_down = 0.5 * (down_ref[rows(1), :] + c_ref[turned(0), :]) * (
        f_ref[turned(0), :] - down_ref[rows(0), :]
    )
    flux_up = 0.5 * (up_ref[rows(1), :] + c_ref[turned(N - 1), :]) * (
        up_ref[rows(0), :] - f_ref[turned(N - 1), :]
    )
    r_ref[turned(0), :] = r_ref[turned(0), :] - flux_down
    r_ref[turned(N - 1), :] = r_ref[turned(N - 1), :] + flux_up
    r0, r1 = forward(lambda k: r_ref[rows(k), :], g_ref, n_ref, m_ref, gr_ref)
    values = [mat_ref[rows(k), :] for k in range(3)]
    replicate(pay_ref, values + [c_ref[rows(0), :], c_ref[rows(N - 1), :], r0, r1], NEAR_X)
    q, e0, e1 = parts_of(maty_ref, 0, 3)
    face = 0.25 * (c_ref[turned(N - 1), :] + up_ref[rows(1), :])
    e0 = e0 + jnp.where(lax.axis_index("gy") == 0, 0.25 * c_ref[turned(0), :], 0.0)
    h = 1.0 / (q + face + e1)
    qh, fh = q * h, face * h
    replicate(elem_ref, (qh * face, e0 + qh * e1, fh * e1, qh, fh, h), 1)


def x_merge_kernel(far, got_ref, pay_ref):
    whole, _ = tree([parts_of(got_ref, i, 7) for i in range(NEAR_X)], join_blocks)
    replicate(pay_ref, whole, far)


def segment(value, s, up):
    return pltpu.roll(value, N - s if up else s, 0)


def matrix_kernel(
    c_ref, g_ref, n_ref, m_ref, mat_ref, gz_ref, nz_ref, mz_ref, matz_ref, cz_ref
):
    cells = [c_ref[turned(k), :] for k in range(N)]
    for k, part in enumerate(eliminated(cells, g_ref, n_ref, m_ref)):
        mat_ref[rows(k), :] = part
    turn(c_ref, cz_ref)
    cells = [cz_ref[turned(k), :] for k in range(N)]
    q, e0, e1 = eliminated(cells, gz_ref, nz_ref, mz_ref)
    place = lax.broadcasted_iota(jnp.int32, (N, LANES), 0) % SEGMENTS
    inside_low, inside_high = place > 0, place < SEGMENTS - 1
    c0, c1 = cells[0], cells[N - 1]
    low = 0.25 * (jnp.where(inside_low, segment(c1, 1, False), 0.0) + c0)
    high = 0.25 * (jnp.where(inside_high, segment(c0, 1, True), 0.0) + c1)
    e0 = e0 + jnp.where(inside_low, 0.0, low)
    e1 = e1 + jnp.where(inside_high, 0.0, high)
    low = jnp.where(inside_low, low, 0.0)
    high = jnp.where(inside_high, high, 0.0)
    h = 1.0 / (q + high + e1)
    qh, eh = q * h, e1 * h
    lower = low * segment(qh, 1, False)
    upper = qh * high
    excess = e0 + q * eh + low * segment(eh, 1, False)
    parts = [h, qh, high * h, low]
    for s in ROUNDS:
        g = 1.0 / (lower + upper + excess)
        before, after = lower * segment(g, s, False), upper * segment(g, s, True)
        parts += [before, after]
        excess = excess + before * segment(excess, s, False) + after * segment(excess, s, True)
        lower, upper = before * segment(lower, s, False), after * segment(upper, s, True)
    for k, part in enumerate(parts + [1.0 / excess]):
        matz_ref[rows(k), :] = part


def turn(from_ref, to_ref):
    for half in range(CELLS // LANES):
        part = pl.ds(LANES * half, LANES)
        to_ref[part, :] = from_ref[part, :].T


def x_back_kernel(
    far, near_ref, all_ref, f_ref, gr_ref, n_ref, m_ref, gy_ref, ny_ref, my_ref, mat_ref, gry_ref, pay_ref, hr_ref, u_ref, ends_ref
):
    me = lax.axis_index("gx")
    whole, ends = tree([parts_of(all_ref, i, 7) for i in range(far)], join_blocks)
    q, e0, e1, c0, c1, r0, r1 = whole
    e0, e1 = e0 + 0.25 * c0, e1 + 0.25 * c1
    h = 1.0 / (q + e1)
    qh = q * h
    u0 = (r0 + qh * r1) / (e0 + qh * e1)
    u0, u1 = chosen(ends(u0, h * r1 + qh * u0), ends_ref, me // NEAR_X)
    _, ends = tree([parts_of(near_ref, i, 7) for i in range(NEAR_X)], join_blocks)
    u0, u1 = chosen(ends(u0, u1), ends_ref, me % NEAR_X)

    def emit(k, w):
        u_ref[rows(k), :] = w - 2.0 * f_ref[rows(k), :]

    backward(u0, u1, gr_ref, n_ref, m_ref, emit)
    r0, r1 = forward(lambda k: u_ref[turned(k), :], gy_ref, ny_ref, my_ref, gry_ref)
    kappa, ea, eb, qh, fh, h = parts_of(mat_ref, 0, 6)
    replicate(pay_ref, (kappa, ea, eb, r0 + qh * r1, fh * r1), NEAR_Y)
    hr_ref[...] = h * r1


def y_merge_kernel(far, got_ref, pay_ref):
    whole, _ = tree([parts_of(got_ref, i, 5) for i in range(NEAR_Y)], join_elements)
    replicate(pay_ref, whole, far)


def y_back_kernel(
    far, near_ref, all_ref, mat_ref, hr_ref, f_ref, gry_ref, ny_ref, my_ref, gz_ref, nz_ref, mz_ref, matz_ref, out_ref, u_ref, ends_ref, uz_ref, grz_ref
):
    me = lax.axis_index("gy")
    (kappa, ea, _, ra, _), ends = tree([parts_of(all_ref, i, 5) for i in range(far)], join_elements)
    u0 = ra / (kappa + ea)
    u0, u1 = chosen(ends(u0, jnp.zeros_like(u0)), ends_ref, me // NEAR_Y)
    _, ends = tree([parts_of(near_ref, i, 5) for i in range(NEAR_Y)], join_elements)
    u0, u_next = chosen(ends(u0, u1), ends_ref, me % NEAR_Y)
    u1 = hr_ref[...] + mat_ref[rows(3), :] * u0 + mat_ref[rows(4), :] * u_next

    def emit_y(k, u):
        u_ref[turned(k), :] = u

    backward(u0, u1, gry_ref, ny_ref, my_ref, emit_y)
    turn(u_ref, uz_ref)
    r0, r1 = forward(lambda k: uz_ref[turned(k), :], gz_ref, nz_ref, mz_ref, grz_ref)
    h, qh, fh, low = parts_of(matz_ref, 0, 4)
    right = r0 + qh * r1 + low * segment(h * r1, 1, False)
    for at, s in enumerate(ROUNDS):
        before, after = matz_ref[rows(4 + 2 * at), :], matz_ref[rows(5 + 2 * at), :]
        right = right + before * segment(right, s, False) + after * segment(right, s, True)
    u0 = right * matz_ref[rows(4 + 2 * len(ROUNDS)), :]
    u1 = h * r1 + qh * u0 + fh * segment(u0, 1, True)

    def emit_z(k, u):
        uz_ref[turned(k), :] = u

    backward(u0, u1, grz_ref, nz_ref, mz_ref, emit_z)
    turn(uz_ref, u_ref)
    out_ref[...] = f_ref[...] + u_ref[...]


def call(kernel, outs, scratch=()):
    return pl.pallas_call(
        kernel,
        out_shape=outs,
        scratch_shapes=[pltpu.VMEM(part, jnp.float32) for part in scratch],
        compiler_params=pltpu.CompilerParams(vmem_limit_bytes=16 * 1024 * 1024),
    )


def gathered(pay, axis, groups):
    count = len(groups[0])
    got = lax.all_to_all(
        pay.reshape(count, -1, LANES), axis, 0, 0, tiled=True, axis_index_groups=groups
    )
    return got.reshape(-1, LANES)


def body(field, conductance, source):
    size_x, size_y = lax.axis_size("gx"), lax.axis_size("gy")
    far_x, far_y = size_x // NEAR_X, size_y // NEAR_Y
    f, c, s = (part.reshape(CELLS, LANES) for part in (field, conductance, source))
    whole, block = shape(CELLS, LANES), (CELLS, LANES)
    everything = jnp.concatenate([f, c, s])
    edge = shape(2 * N, LANES)
    outer, inner = call(edges_kernel, (edge, edge))(everything)
    across = [(i, i + 1) for i in range(1, size_y - 1, 2)]
    across += [(b, a) for a, b in across]
    outer = lax.ppermute(outer, "gy", across)
    inner = lax.ppermute(inner, "gy", [(i, i ^ 1) for i in range(size_y)])
    f, c, rhs, gx, nx, mx, mat_x = call(
        prepare_kernel, (whole, whole, whole, whole, whole, whole, shape(3 * N, LANES)), [block]
    )(everything)
    gy, ny, my, mat_y, gz, nz, mz, mat_z = call(
        matrix_kernel,
        (whole, whole, whole, shape(3 * N, LANES), whole, whole, whole)
        + (shape((5 + 2 * len(ROUNDS)) * N, LANES),),
        [block],
    )(c)
    grx, pay, mat_y = call(
        x_forward_kernel, (whole, shape(NEAR_X * 7 * N, LANES), shape(6 * N, LANES)), [block, (2 * N, LANES), (2 * N, LANES)]
    )(f, c, rhs, gx, nx, mx, mat_x, mat_y, outer, inner)
    near = gathered(pay, "gx", [[NEAR_X * i + j for j in range(NEAR_X)] for i in range(far_x)])
    pay = call(lambda *refs: x_merge_kernel(far_x, *refs), shape(far_x * 7 * N, LANES))(near)
    every = gathered(pay, "gx", [[NEAR_X * i + j for i in range(far_x)] for j in range(NEAR_X)])
    gry, pay, hr = call(
        lambda *refs: x_back_kernel(far_x, *refs),
        (whole, shape(NEAR_Y * 5 * N, LANES), shape(N, LANES)),
        [block, (2 * max(far_x, NEAR_X) * N, LANES)],
    )(near, every, f, grx, nx, mx, gy, ny, my, mat_y)
    near = gathered(pay, "gy", [[NEAR_Y * i + j for j in range(NEAR_Y)] for i in range(far_y)])
    pay = call(lambda *refs: y_merge_kernel(far_y, *refs), shape(far_y * 5 * N, LANES))(near)
    every = gathered(pay, "gy", [[NEAR_Y * i + j for i in range(far_y)] for j in range(NEAR_Y)])
    out = call(
        lambda *refs: y_back_kernel(far_y, *refs), whole, [block, (2 * max(far_y, NEAR_Y) * N, LANES), block, block]
    )(near, every, mat_y, hr, f, gry, ny, my, gz, nz, mz, mat_z)
    return out.reshape(field.shape)


def solution(mesh):
    spec = P("gx", "gy", None)
    return jax.shard_map(
        body, mesh=mesh, in_specs=(spec, spec, spec), out_specs=spec, check_vma=False
    )
```

```python
import jax
import jax.numpy as jnp
from jax import lax
from jax.experimental import pallas as pl
from jax.experimental.pallas import tpu as pltpu
from jax.sharding import PartitionSpec as P

N = 16
CELLS = N * N
LANES = 128
SEGMENTS = LANES // N
ROUNDS = (1, 2, 4)
NEAR_X = 8
BLOCK = 7 * N + 8
NEAR_Y = 4


def rows(k):
    return pl.ds(N * k, N)


def turned(k):
    return pl.ds(k, N, stride=N)


def row(k):
    return pl.ds(k, 1)


def shape(*dims):
    return jax.ShapeDtypeStruct(dims, jnp.float32)


def eliminated(cells, g_ref, n_ref, m_ref, at=rows):
    one = jnp.ones_like(cells[0])
    half = [None] + [0.25 * (cells[k - 1] + cells[k]) for k in range(1, N)]
    first, excess, excess_first = half[1], one, one
    for k in range(1, N - 1):
        g = 1.0 / (first + half[k + 1] + excess)
        n = first * g
        m = half[k + 1] * g
        g_ref[at(k), :] = g
        n_ref[at(k), :] = n
        m_ref[at(k + 1), :] = m
        excess_first = excess_first + n * excess
        first = m * first
        excess = one + m * excess
    return first, excess_first, excess


def forward(right, g_ref, n_ref, m_ref, gr_ref, at=rows):
    r0, carried = right(0), None
    for k in range(1, N):
        carried = right(k) if carried is None else right(k) + m_ref[at(k), :] * carried
        if k < N - 1:
            r0 = r0 + n_ref[at(k), :] * carried
            gr_ref[at(k), :] = g_ref[at(k), :] * carried
    return r0, carried


def backward(u0, u1, gr_ref, n_ref, m_ref, emit, at=rows):
    emit(0, u0)
    emit(N - 1, u1)
    later = u1
    for k in range(N - 2, 0, -1):
        later = gr_ref[at(k), :] + n_ref[at(k), :] * u0 + m_ref[at(k + 1), :] * later
        emit(k, later)


def join_blocks(left, right):
    ql, e0l, e1l, c0l, c1l, r0l, r1l = left
    qr, e0r, e1r, c0r, c1r, r0r, r1r = right
    face = 0.25 * (c1l + c0r)
    h = 1.0 / (ql + face + e1l)
    s, t = face * h, ql * h
    p = s * ql
    ew = e0r + s * e1l
    rw = r0r + s * r1l
    k = 1.0 / (qr + p + ew)
    qk, pk = qr * k, p * k
    joined = (
        qk * p, e0l + t * e1l + pk * ew, e1r + qk * ew, c0l, c1r, r0l + t * r1l + pk * rw, r1r + qk * rw
    )

    def expand(u0, u1):
        w = k * rw + qk * u1 + pk * u0
        return (u0, h * r1l + t * u0 + s * w), (w, u1)

    return joined, expand


def join_elements(left, right):
    kl, eal, ebl, ral, rbl = left
    kr, ear, ebr, rar, rbr = right
    em, rm = ebl + ear, rbl + rar
    k = 1.0 / (kl + kr + em)
    lk, rk = kl * k, kr * k
    joined = (lk * kr, eal + lk * em, ebr + rk * em, ral + lk * rm, rbr + rk * rm)

    def expand(u0, u1):
        middle = k * rm + lk * u0 + rk * u1
        return (u0, middle), (middle, u1)

    return joined, expand


def tree(parts, join):
    levels = []
    while len(parts) > 1:
        pairs = [join(parts[i], parts[i + 1]) for i in range(0, len(parts), 2)]
        levels.append([expand for _, expand in pairs])
        parts = [joined for joined, _ in pairs]

    def ends(u0, u1):
        found = [(u0, u1)]
        for expands in reversed(levels):
            found = [end for expand, both in zip(expands, found) for end in expand(*both)]
        return found

    return parts[0], ends


def chosen(found, scratch_ref, index, count=N):
    for i, (u0, u1) in enumerate(found):
        scratch_ref[pl.ds(2 * N * i, count), :] = u0
        scratch_ref[pl.ds(2 * N * i + N, count), :] = u1
    start = pl.multiple_of(index * 2 * N, 2 * N)
    return scratch_ref[pl.ds(start, count), :], scratch_ref[pl.ds(start + N, count), :]


def parts_of(ref, i, count):
    return tuple(ref[rows(count * i + k), :] for k in range(count))


def replicate(pay_ref, values, copies):
    for i in range(copies):
        for k, value in enumerate(values):
            pay_ref[rows(len(values) * i + k), :] = value


def block_of(ref, i):
    return tuple(ref[pl.ds(BLOCK * i + N * k, N), :] for k in range(7))


def extra_of(ref, i):
    return tuple(ref[row(BLOCK * i + 7 * N + k), :] for k in range(7))


def replicate_blocks(pay_ref, values, extra, copies):
    for i in range(copies):
        for k, value in enumerate(values):
            pay_ref[pl.ds(BLOCK * i + N * k, N), :] = value
        for k, value in enumerate(extra + (jnp.zeros_like(extra[0]),)):
            pay_ref[row(BLOCK * i + 7 * N + k), :] = value


def edges_kernel(all_ref, last_ref):
    for at in (0, 1):
        last_ref[rows(at), :] = all_ref[pl.ds(CELLS * at + N - 1, N, stride=N), :]


def prepare_kernel(size_y, all_ref, f_ref, c_ref, rhs_ref, g_ref, n_ref, m_ref, mat_ref, ay_ref):
    f_ref[...] = all_ref[pl.ds(0, CELLS), :]
    c_ref[...] = all_ref[pl.ds(CELLS, CELLS), :]
    cells = [all_ref[rows(N + k), :] for k in range(N)]
    for k, part in enumerate(eliminated(cells, g_ref, n_ref, m_ref)):
        mat_ref[rows(k), :] = part
    flux = None
    for y in range(N - 1):
        c0, c1 = c_ref[turned(y), :], c_ref[turned(y + 1), :]
        f0, f1 = f_ref[turned(y), :], f_ref[turned(y + 1), :]
        after = 0.5 * (c0 + c1) * (f1 - f0)
        ay_ref[turned(y), :] = after if flux is None else after - flux
        flux = after
    top = lax.axis_index("gy") == size_y - 1
    ay_ref[turned(N - 1), :] = -flux - jnp.where(top, 0.5 * c1 * f1, 0.0)
    lane = lax.broadcasted_iota(jnp.int32, (N, LANES), 1)
    for k in range(N):
        c, f = cells[k], f_ref[rows(k), :]
        c_next = jnp.where(lane < LANES - 1, pltpu.roll(c, LANES - 1, 1), 0.0)
        f_next = jnp.where(lane < LANES - 1, pltpu.roll(f, LANES - 1, 1), 0.0)
        upper = 0.5 * (c + c_next) * (f_next - f)
        lower = jnp.where(lane > 0, pltpu.roll(upper, 1, 1), 0.5 * c * f)
        rhs_ref[rows(k), :] = 2.0 * f + all_ref[rows(2 * N + k), :] + ay_ref[rows(k), :] + (upper - lower)


def x_forward_kernel(
    size_y, f_ref, c_ref, rhs_ref, g_ref, n_ref, m_ref, mat_ref, maty_ref, down_ref, gr_ref, pay_ref, elem_ref, gre_ref, ne_ref, me_ref, r_ref, ge_ref, flux_ref
):
    r_ref[...] = rhs_ref[...]
    first, last, below = c_ref[turned(0), :], c_ref[turned(N - 1), :], down_ref[rows(1), :]
    flux = 0.5 * (below + first) * (f_ref[turned(0), :] - down_ref[rows(0), :])
    r_ref[turned(0), :] = r_ref[turned(0), :] - flux
    flux_ref[...] = flux
    r0, r1 = forward(lambda k: r_ref[rows(k), :], g_ref, n_ref, m_ref, gr_ref)
    values = parts_of(mat_ref, 0, 3) + (c_ref[rows(0), :], c_ref[rows(N - 1), :], r0, r1)
    cells = [down_ref[row(N + k), :] for k in range(N)]
    extra = eliminated(cells, ge_ref, ne_ref, me_ref, row) + (cells[0], cells[N - 1])
    extra += forward(lambda k: flux_ref[row(k), :], ge_ref, ne_ref, me_ref, gre_ref, row)
    replicate_blocks(pay_ref, values, extra, NEAR_X)
    q, e0, e1 = parts_of(maty_ref, 0, 3)
    e1 = e1 + jnp.where(lax.axis_index("gy") == size_y - 1, 0.25 * last, 0.0)
    face = 0.25 * (below + first)
    h = 1.0 / (q + face + e0)
    qh, fh = q * h, face * h
    replicate(elem_ref, (qh * face, fh * e0, e1 + qh * e0, qh, fh, h), 1)


def x_merge_kernel(far, got_ref, pay_ref):
    whole, _ = tree([block_of(got_ref, i) for i in range(NEAR_X)], join_blocks)
    extra, _ = tree([extra_of(got_ref, i) for i in range(NEAR_X)], join_blocks)
    replicate_blocks(pay_ref, whole, extra, far)


def segment(value, s, up):
    return pltpu.roll(value, N - s if up else s, 0)


def matrix_kernel(
    c_ref, g_ref, n_ref, m_ref, mat_ref, gz_ref, nz_ref, mz_ref, matz_ref, cz_ref
):
    cells = [c_ref[turned(k), :] for k in range(N)]
    for k, part in enumerate(eliminated(cells, g_ref, n_ref, m_ref)):
        mat_ref[rows(k), :] = part
    turn(c_ref, cz_ref)
    cells = [cz_ref[turned(k), :] for k in range(N)]
    q, e0, e1 = eliminated(cells, gz_ref, nz_ref, mz_ref)
    place = lax.broadcasted_iota(jnp.int32, (N, LANES), 0) % SEGMENTS
    inside_low, inside_high = place > 0, place < SEGMENTS - 1
    c0, c1 = cells[0], cells[N - 1]
    low = 0.25 * (jnp.where(inside_low, segment(c1, 1, False), 0.0) + c0)
    high = 0.25 * (jnp.where(inside_high, segment(c0, 1, True), 0.0) + c1)
    e0 = e0 + jnp.where(inside_low, 0.0, low)
    e1 = e1 + jnp.where(inside_high, 0.0, high)
    low = jnp.where(inside_low, low, 0.0)
    high = jnp.where(inside_high, high, 0.0)
    h = 1.0 / (q + high + e1)
    qh, eh = q * h, e1 * h
    lower = low * segment(qh, 1, False)
    upper = qh * high
    excess = e0 + q * eh + low * segment(eh, 1, False)
    parts = [h, qh, high * h, low]
    for s in ROUNDS:
        g = 1.0 / (lower + upper + excess)
        before, after = lower * segment(g, s, False), upper * segment(g, s, True)
        parts += [before, after]
        excess = excess + before * segment(excess, s, False) + after * segment(excess, s, True)
        lower, upper = before * segment(lower, s, False), after * segment(upper, s, True)
    for k, part in enumerate(parts + [1.0 / excess]):
        matz_ref[rows(k), :] = part


def turn(from_ref, to_ref):
    for half in range(CELLS // LANES):
        part = pl.ds(LANES * half, LANES)
        to_ref[part, :] = from_ref[part, :].T


def x_ends(far, near_ref, all_ref, part_of, ends_ref, count):
    me = lax.axis_index("gx")
    whole, ends = tree([part_of(all_ref, i) for i in range(far)], join_blocks)
    q, e0, e1, c0, c1, r0, r1 = whole
    e0, e1 = e0 + 0.25 * c0, e1 + 0.25 * c1
    h = 1.0 / (q + e1)
    qh = q * h
    u0 = (r0 + qh * r1) / (e0 + qh * e1)
    u0, u1 = chosen(ends(u0, h * r1 + qh * u0), ends_ref, me // NEAR_X, count)
    _, ends = tree([part_of(near_ref, i) for i in range(NEAR_X)], join_blocks)
    return chosen(ends(u0, u1), ends_ref, me % NEAR_X, count)


def x_back_kernel(
    far, near_ref, all_ref, f_ref, gr_ref, n_ref, m_ref, gre_ref, ne_ref, me_ref, gy_ref, ny_ref, my_ref, mat_ref, gry_ref, pay_ref, hr_ref, u_ref, ends_ref, endse_ref, below_ref
):
    u0, u1 = x_ends(far, near_ref, all_ref, block_of, ends_ref, N)
    v0, v1 = x_ends(far, near_ref, all_ref, extra_of, endse_ref, 1)

    def emit(k, w):
        u_ref[rows(k), :] = w - 2.0 * f_ref[rows(k), :]

    def emit_below(k, w):
        below_ref[row(k), :] = w

    backward(u0, u1, gr_ref, n_ref, m_ref, emit)
    backward(v0, v1, gre_ref, ne_ref, me_ref, emit_below, row)
    r0, r1 = forward(lambda k: u_ref[turned(k), :], gy_ref, ny_ref, my_ref, gry_ref)
    kappa, ea, eb, qh, fh, h = parts_of(mat_ref, 0, 6)
    replicate(pay_ref, (kappa, ea, eb, fh * r0 + below_ref[...], r1 + qh * r0), NEAR_Y)
    hr_ref[...] = h * r0


def y_merge_kernel(far, got_ref, pay_ref):
    whole, _ = tree([parts_of(got_ref, i, 5) for i in range(NEAR_Y)], join_elements)
    replicate(pay_ref, whole, far)


def y_back_kernel(
    far, near_ref, all_ref, mat_ref, hr_ref, f_ref, gry_ref, ny_ref, my_ref, gz_ref, nz_ref, mz_ref, matz_ref, out_ref, u_ref, ends_ref, uz_ref, grz_ref
):
    me = lax.axis_index("gy")
    (kappa, _, eb, _, rb), ends = tree([parts_of(all_ref, i, 5) for i in range(far)], join_elements)
    u1 = rb / (kappa + eb)
    u0, u1 = chosen(ends(jnp.zeros_like(u1), u1), ends_ref, me // NEAR_Y)
    _, ends = tree([parts_of(near_ref, i, 5) for i in range(NEAR_Y)], join_elements)
    below, u1 = chosen(ends(u0, u1), ends_ref, me % NEAR_Y)
    u0 = hr_ref[...] + mat_ref[rows(3), :] * u1 + mat_ref[rows(4), :] * below

    def emit_y(k, u):
        u_ref[turned(k), :] = u

    backward(u0, u1, gry_ref, ny_ref, my_ref, emit_y)
    turn(u_ref, uz_ref)
    r0, r1 = forward(lambda k: uz_ref[turned(k), :], gz_ref, nz_ref, mz_ref, grz_ref)
    h, qh, fh, low = parts_of(matz_ref, 0, 4)
    right = r0 + qh * r1 + low * segment(h * r1, 1, False)
    for at, s in enumerate(ROUNDS):
        before, after = matz_ref[rows(4 + 2 * at), :], matz_ref[rows(5 + 2 * at), :]
        right = right + before * segment(right, s, False) + after * segment(right, s, True)
    u0 = right * matz_ref[rows(4 + 2 * len(ROUNDS)), :]
    u1 = h * r1 + qh * u0 + fh * segment(u0, 1, True)

    def emit_z(k, u):
        uz_ref[turned(k), :] = u

    backward(u0, u1, grz_ref, nz_ref, mz_ref, emit_z)
    turn(uz_ref, u_ref)
    out_ref[...] = f_ref[...] + u_ref[...]


def call(kernel, outs, scratch=()):
    return pl.pallas_call(
        kernel,
        out_shape=outs,
        scratch_shapes=[pltpu.VMEM(part, jnp.float32) for part in scratch],
        compiler_params=pltpu.CompilerParams(vmem_limit_bytes=16 * 1024 * 1024),
    )


def gathered(pay, axis, groups):
    count = len(groups[0])
    got = lax.all_to_all(
        pay.reshape(count, -1, LANES), axis, 0, 0, tiled=True, axis_index_groups=groups
    )
    return got.reshape(-1, LANES)


def body(field, conductance, source):
    size_x, size_y = lax.axis_size("gx"), lax.axis_size("gy")
    far_x, far_y = size_x // NEAR_X, size_y // NEAR_Y
    f, c, s = (part.reshape(CELLS, LANES) for part in (field, conductance, source))
    whole, block = shape(CELLS, LANES), (CELLS, LANES)
    everything = jnp.concatenate([f, c, s])
    last = call(edges_kernel, shape(2 * N, LANES))(everything)
    down = lax.ppermute(last, "gy", [(i, i + 1) for i in range(size_y - 1)])
    f, c, rhs, gx, nx, mx, mat_x = call(
        lambda *refs: prepare_kernel(size_y, *refs), (whole, whole, whole, whole, whole, whole, shape(3 * N, LANES)), [block]
    )(everything)
    gy, ny, my, mat_y, gz, nz, mz, mat_z = call(
        matrix_kernel,
        (whole, whole, whole, shape(3 * N, LANES), whole, whole, whole)
        + (shape((5 + 2 * len(ROUNDS)) * N, LANES),),
        [block],
    )(c)
    line = shape(N, LANES)
    grx, pay, mat_y, gre, ne, me = call(
        lambda *refs: x_forward_kernel(size_y, *refs),
        (whole, shape(NEAR_X * BLOCK, LANES), shape(6 * N, LANES), line, line, line),
        [block, (N, LANES), (N, LANES)],
    )(f, c, rhs, gx, nx, mx, mat_x, mat_y, down)
    near = gathered(pay, "gx", [[NEAR_X * i + j for j in range(NEAR_X)] for i in range(far_x)])
    pay = call(lambda *refs: x_merge_kernel(far_x, *refs), shape(far_x * BLOCK, LANES))(near)
    every = gathered(pay, "gx", [[NEAR_X * i + j for i in range(far_x)] for j in range(NEAR_X)])
    ends = (2 * max(far_x, NEAR_X) * N, LANES)
    gry, pay, hr = call(
        lambda *refs: x_back_kernel(far_x, *refs),
        (whole, shape(NEAR_Y * 5 * N, LANES), shape(N, LANES)),
        [block, ends, ends, (N, LANES)],
    )(near, every, f, grx, nx, mx, gre, ne, me, gy, ny, my, mat_y)
    near = gathered(pay, "gy", [[NEAR_Y * i + j for j in range(NEAR_Y)] for i in range(far_y)])
    pay = call(lambda *refs: y_merge_kernel(far_y, *refs), shape(far_y * 5 * N, LANES))(near)
    every = gathered(pay, "gy", [[NEAR_Y * i + j for i in range(far_y)] for j in range(NEAR_Y)])
    out = call(
        lambda *refs: y_back_kernel(far_y, *refs), whole, [block, (2 * max(far_y, NEAR_Y) * N, LANES), block, block]
    )(near, every, mat_y, hr, f, gry, ny, my, gz, nz, mz, mat_z)
    return out.reshape(field.shape)


def solution(mesh):
    spec = P("gx", "gy", None)
    return jax.shard_map(
        body, mesh=mesh, in_specs=(spec, spec, spec), out_specs=spec, check_vma=False
    )
```

```python
import jax
import jax.numpy as jnp
from jax import lax
from jax.experimental import pallas as pl
from jax.experimental.pallas import tpu as pltpu
from jax.sharding import PartitionSpec as P

N = 16
CELLS = N * N
LANES = 128
SEGMENTS = LANES // N
ROUNDS = (1, 2, 4)
NEAR_X = 8
BLOCK = 5 * N + 8
NEAR_Y = 4


def rows(k):
    return pl.ds(N * k, N)


def turned(k):
    return pl.ds(k, N, stride=N)


def row(k):
    return pl.ds(k, 1)


def shape(*dims):
    return jax.ShapeDtypeStruct(dims, jnp.float32)


def eliminated(cells, g_ref, n_ref, m_ref, at=rows):
    one = jnp.ones_like(cells[0])
    half = [None] + [0.25 * (cells[k - 1] + cells[k]) for k in range(1, N)]
    first, excess, excess_first = half[1], one, one
    for k in range(1, N - 1):
        g = 1.0 / (first + half[k + 1] + excess)
        n = first * g
        m = half[k + 1] * g
        g_ref[at(k), :] = g
        n_ref[at(k), :] = n
        m_ref[at(k + 1), :] = m
        excess_first = excess_first + n * excess
        first = m * first
        excess = one + m * excess
    return first, excess_first, excess


def forward(right, g_ref, n_ref, m_ref, gr_ref, at=rows):
    r0, carried = right(0), None
    for k in range(1, N):
        carried = right(k) if carried is None else right(k) + m_ref[at(k), :] * carried
        if k < N - 1:
            r0 = r0 + n_ref[at(k), :] * carried
            gr_ref[at(k), :] = g_ref[at(k), :] * carried
    return r0, carried


def backward(u0, u1, gr_ref, n_ref, m_ref, emit, at=rows):
    emit(0, u0)
    emit(N - 1, u1)
    later = u1
    for k in range(N - 2, 0, -1):
        later = gr_ref[at(k), :] + n_ref[at(k), :] * u0 + m_ref[at(k + 1), :] * later
        emit(k, later)


def join_blocks(left, right):
    ql, e0l, e1l, c0l, c1l, r0l, r1l = left
    qr, e0r, e1r, c0r, c1r, r0r, r1r = right
    face = 0.25 * (c1l + c0r)
    h = 1.0 / (ql + face + e1l)
    s, t = face * h, ql * h
    p = s * ql
    ew = e0r + s * e1l
    rw = r0r + s * r1l
    k = 1.0 / (qr + p + ew)
    qk, pk = qr * k, p * k
    joined = (
        qk * p, e0l + t * e1l + pk * ew, e1r + qk * ew, c0l, c1r, r0l + t * r1l + pk * rw, r1r + qk * rw
    )

    def expand(u0, u1):
        w = k * rw + qk * u1 + pk * u0
        return (u0, h * r1l + t * u0 + s * w), (w, u1)

    return joined, expand


def join_elements(left, right):
    kl, eal, ebl, ral, rbl = left
    kr, ear, ebr, rar, rbr = right
    em, rm = ebl + ear, rbl + rar
    k = 1.0 / (kl + kr + em)
    lk, rk = kl * k, kr * k
    joined = (lk * kr, eal + lk * em, ebr + rk * em, ral + lk * rm, rbr + rk * rm)

    def expand(u0, u1):
        middle = k * rm + lk * u0 + rk * u1
        return (u0, middle), (middle, u1)

    return joined, expand


def tree(parts, join):
    levels = []
    while len(parts) > 1:
        pairs = [join(parts[i], parts[i + 1]) for i in range(0, len(parts), 2)]
        levels.append([expand for _, expand in pairs])
        parts = [joined for joined, _ in pairs]

    def ends(u0, u1):
        found = [(u0, u1)]
        for expands in reversed(levels):
            found = [end for expand, both in zip(expands, found) for end in expand(*both)]
        return found

    return parts[0], ends


def chosen(found, scratch_ref, index, count=N):
    for i, (u0, u1) in enumerate(found):
        scratch_ref[pl.ds(2 * N * i, count), :] = u0
        scratch_ref[pl.ds(2 * N * i + N, count), :] = u1
    start = pl.multiple_of(index * 2 * N, 2 * N)
    return scratch_ref[pl.ds(start, count), :], scratch_ref[pl.ds(start + N, count), :]


def parts_of(ref, i, count):
    return tuple(ref[rows(count * i + k), :] for k in range(count))


def replicate(pay_ref, values, copies):
    for i in range(copies):
        for k, value in enumerate(values):
            pay_ref[rows(len(values) * i + k), :] = value


def block_of(ref, i):
    return tuple(ref[pl.ds(BLOCK * i + N * k, N), :] for k in range(5))


def extra_of(ref, i):
    return tuple(ref[row(BLOCK * i + 5 * N + k), :] for k in range(7))


def replicate_blocks(pay_ref, values, extra, copies):
    for i in range(copies):
        for k, value in enumerate(values):
            pay_ref[pl.ds(BLOCK * i + N * k, N), :] = value
        for k, value in enumerate(extra + (jnp.zeros_like(extra[0]),)):
            pay_ref[row(BLOCK * i + 5 * N + k), :] = value


def edges_kernel(all_ref, last_ref, front_ref):
    front_ref[...] = all_ref[rows(N), :]
    for at in (0, 1):
        last_ref[rows(at), :] = all_ref[pl.ds(CELLS * at + N - 1, N, stride=N), :]


def prepare_kernel(size_y, all_ref, f_ref, c_ref, rhs_ref, g_ref, n_ref, m_ref, mat_ref, ay_ref):
    f_ref[...] = all_ref[pl.ds(0, CELLS), :]
    c_ref[...] = all_ref[pl.ds(CELLS, CELLS), :]
    cells = [all_ref[rows(N + k), :] for k in range(N)]
    for k, part in enumerate(eliminated(cells, g_ref, n_ref, m_ref)):
        mat_ref[rows(k), :] = part
    flux = None
    for y in range(N - 1):
        c0, c1 = c_ref[turned(y), :], c_ref[turned(y + 1), :]
        f0, f1 = f_ref[turned(y), :], f_ref[turned(y + 1), :]
        after = 0.5 * (c0 + c1) * (f1 - f0)
        ay_ref[turned(y), :] = after if flux is None else after - flux
        flux = after
    top = lax.axis_index("gy") == size_y - 1
    ay_ref[turned(N - 1), :] = -flux - jnp.where(top, 0.5 * c1 * f1, 0.0)
    lane = lax.broadcasted_iota(jnp.int32, (N, LANES), 1)
    for k in range(N):
        c, f = cells[k], f_ref[rows(k), :]
        c_next = jnp.where(lane < LANES - 1, pltpu.roll(c, LANES - 1, 1), 0.0)
        f_next = jnp.where(lane < LANES - 1, pltpu.roll(f, LANES - 1, 1), 0.0)
        upper = 0.5 * (c + c_next) * (f_next - f)
        lower = jnp.where(lane > 0, pltpu.roll(upper, 1, 1), 0.5 * c * f)
        rhs_ref[rows(k), :] = 2.0 * f + all_ref[rows(2 * N + k), :] + ay_ref[rows(k), :] + (upper - lower)


def x_forward_kernel(
    size_y, f_ref, c_ref, rhs_ref, g_ref, n_ref, m_ref, mat_ref, maty_ref, down_ref, next_ref, gr_ref, pay_ref, elem_ref, elemx_ref, gre_ref, ne_ref, me_ref, r_ref, ge_ref, flux_ref
):
    r_ref[...] = rhs_ref[...]
    first, last, below = c_ref[turned(0), :], c_ref[turned(N - 1), :], down_ref[rows(1), :]
    flux = 0.5 * (below + first) * (f_ref[turned(0), :] - down_ref[rows(0), :])
    r_ref[turned(0), :] = r_ref[turned(0), :] - flux
    flux_ref[...] = flux
    r0, r1 = forward(lambda k: r_ref[rows(k), :], g_ref, n_ref, m_ref, gr_ref)
    q, e0, e1 = parts_of(mat_ref, 0, 3)
    e0 = e0 + jnp.where(lax.axis_index("gx") == 0, 0.25 * c_ref[rows(0), :], 0.0)
    face = 0.25 * (c_ref[rows(N - 1), :] + next_ref[...])
    h = 1.0 / (q + face + e1)
    qh, fh = q * h, face * h
    values = (qh * face, e0 + qh * e1, fh * e1, r0 + qh * r1, fh * r1)
    replicate(elemx_ref, (qh, fh, h * r1), 1)
    cells = [down_ref[row(N + k), :] for k in range(N)]
    extra = eliminated(cells, ge_ref, ne_ref, me_ref, row) + (cells[0], cells[N - 1])
    extra += forward(lambda k: flux_ref[row(k), :], ge_ref, ne_ref, me_ref, gre_ref, row)
    replicate_blocks(pay_ref, values, extra, NEAR_X)
    q, e0, e1 = parts_of(maty_ref, 0, 3)
    e1 = e1 + jnp.where(lax.axis_index("gy") == size_y - 1, 0.25 * last, 0.0)
    face = 0.25 * (below + first)
    h = 1.0 / (q + face + e0)
    qh, fh = q * h, face * h
    replicate(elem_ref, (qh * face, fh * e0, e1 + qh * e0, qh, fh, h), 1)


def x_merge_kernel(far, got_ref, pay_ref):
    whole, _ = tree([block_of(got_ref, i) for i in range(NEAR_X)], join_elements)
    extra, _ = tree([extra_of(got_ref, i) for i in range(NEAR_X)], join_blocks)
    replicate_blocks(pay_ref, whole, extra, far)


def segment(value, s, up):
    return pltpu.roll(value, N - s if up else s, 0)


def matrix_kernel(
    c_ref, g_ref, n_ref, m_ref, mat_ref, gz_ref, nz_ref, mz_ref, matz_ref, cz_ref
):
    cells = [c_ref[turned(k), :] for k in range(N)]
    for k, part in enumerate(eliminated(cells, g_ref, n_ref, m_ref)):
        mat_ref[rows(k), :] = part
    turn(c_ref, cz_ref)
    cells = [cz_ref[turned(k), :] for k in range(N)]
    q, e0, e1 = eliminated(cells, gz_ref, nz_ref, mz_ref)
    place = lax.broadcasted_iota(jnp.int32, (N, LANES), 0) % SEGMENTS
    inside_low, inside_high = place > 0, place < SEGMENTS - 1
    c0, c1 = cells[0], cells[N - 1]
    low = 0.25 * (jnp.where(inside_low, segment(c1, 1, False), 0.0) + c0)
    high = 0.25 * (jnp.where(inside_high, segment(c0, 1, True), 0.0) + c1)
    e0 = e0 + jnp.where(inside_low, 0.0, low)
    e1 = e1 + jnp.where(inside_high, 0.0, high)
    low = jnp.where(inside_low, low, 0.0)
    high = jnp.where(inside_high, high, 0.0)
    h = 1.0 / (q + high + e1)
    qh, eh = q * h, e1 * h
    lower = low * segment(qh, 1, False)
    upper = qh * high
    excess = e0 + q * eh + low * segment(eh, 1, False)
    parts = [h, qh, high * h, low]
    for s in ROUNDS:
        g = 1.0 / (lower + upper + excess)
        before, after = lower * segment(g, s, False), upper * segment(g, s, True)
        parts += [before, after]
        excess = excess + before * segment(excess, s, False) + after * segment(excess, s, True)
        lower, upper = before * segment(lower, s, False), after * segment(upper, s, True)
    for k, part in enumerate(parts + [1.0 / excess]):
        matz_ref[rows(k), :] = part


def turn(from_ref, to_ref):
    for half in range(CELLS // LANES):
        part = pl.ds(LANES * half, LANES)
        to_ref[part, :] = from_ref[part, :].T


def x_ends(far, near_ref, all_ref, part_of, ends_ref, count):
    me = lax.axis_index("gx")
    whole, ends = tree([part_of(all_ref, i) for i in range(far)], join_blocks)
    q, e0, e1, c0, c1, r0, r1 = whole
    e0, e1 = e0 + 0.25 * c0, e1 + 0.25 * c1
    h = 1.0 / (q + e1)
    qh = q * h
    u0 = (r0 + qh * r1) / (e0 + qh * e1)
    u0, u1 = chosen(ends(u0, h * r1 + qh * u0), ends_ref, me // NEAR_X, count)
    _, ends = tree([part_of(near_ref, i) for i in range(NEAR_X)], join_blocks)
    return chosen(ends(u0, u1), ends_ref, me % NEAR_X, count)


def x_element_ends(far, near_ref, all_ref, ends_ref):
    me = lax.axis_index("gx")
    (kappa, ea, _, ra, _), ends = tree([block_of(all_ref, i) for i in range(far)], join_elements)
    u0 = ra / (kappa + ea)
    u0, u1 = chosen(ends(u0, jnp.zeros_like(u0)), ends_ref, me // NEAR_X)
    _, ends = tree([block_of(near_ref, i) for i in range(NEAR_X)], join_elements)
    return chosen(ends(u0, u1), ends_ref, me % NEAR_X)


def x_back_kernel(
    far, near_ref, all_ref, elemx_ref, f_ref, gr_ref, n_ref, m_ref, gre_ref, ne_ref, me_ref, gy_ref, ny_ref, my_ref, mat_ref, gry_ref, pay_ref, hr_ref, u_ref, ends_ref, endse_ref, below_ref
):
    u0, u_next = x_element_ends(far, near_ref, all_ref, ends_ref)
    qh, fh, hr = parts_of(elemx_ref, 0, 3)
    u1 = hr + qh * u0 + fh * u_next
    v0, v1 = x_ends(far, near_ref, all_ref, extra_of, endse_ref, 1)

    def emit(k, w):
        u_ref[rows(k), :] = w - 2.0 * f_ref[rows(k), :]

    def emit_below(k, w):
        below_ref[row(k), :] = w

    backward(u0, u1, gr_ref, n_ref, m_ref, emit)
    backward(v0, v1, gre_ref, ne_ref, me_ref, emit_below, row)
    r0, r1 = forward(lambda k: u_ref[turned(k), :], gy_ref, ny_ref, my_ref, gry_ref)
    kappa, ea, eb, qh, fh, h = parts_of(mat_ref, 0, 6)
    replicate(pay_ref, (kappa, ea, eb, fh * r0 + below_ref[...], r1 + qh * r0), NEAR_Y)
    hr_ref[...] = h * r0


def y_merge_kernel(far, got_ref, pay_ref):
    whole, _ = tree([parts_of(got_ref, i, 5) for i in range(NEAR_Y)], join_elements)
    replicate(pay_ref, whole, far)


def y_back_kernel(
    far, near_ref, all_ref, mat_ref, hr_ref, f_ref, gry_ref, ny_ref, my_ref, gz_ref, nz_ref, mz_ref, matz_ref, out_ref, u_ref, ends_ref, uz_ref, grz_ref
):
    me = lax.axis_index("gy")
    (kappa, _, eb, _, rb), ends = tree([parts_of(all_ref, i, 5) for i in range(far)], join_elements)
    u1 = rb / (kappa + eb)
    u0, u1 = chosen(ends(jnp.zeros_like(u1), u1), ends_ref, me // NEAR_Y)
    _, ends = tree([parts_of(near_ref, i, 5) for i in range(NEAR_Y)], join_elements)
    below, u1 = chosen(ends(u0, u1), ends_ref, me % NEAR_Y)
    u0 = hr_ref[...] + mat_ref[rows(3), :] * u1 + mat_ref[rows(4), :] * below

    def emit_y(k, u):
        u_ref[turned(k), :] = u

    backward(u0, u1, gry_ref, ny_ref, my_ref, emit_y)
    turn(u_ref, uz_ref)
    r0, r1 = forward(lambda k: uz_ref[turned(k), :], gz_ref, nz_ref, mz_ref, grz_ref)
    h, qh, fh, low = parts_of(matz_ref, 0, 4)
    right = r0 + qh * r1 + low * segment(h * r1, 1, False)
    for at, s in enumerate(ROUNDS):
        before, after = matz_ref[rows(4 + 2 * at), :], matz_ref[rows(5 + 2 * at), :]
        right = right + before * segment(right, s, False) + after * segment(right, s, True)
    u0 = right * matz_ref[rows(4 + 2 * len(ROUNDS)), :]
    u1 = h * r1 + qh * u0 + fh * segment(u0, 1, True)

    def emit_z(k, u):
        uz_ref[turned(k), :] = u

    backward(u0, u1, grz_ref, nz_ref, mz_ref, emit_z)
    turn(uz_ref, u_ref)
    out_ref[...] = f_ref[...] + u_ref[...]


def call(kernel, outs, scratch=()):
    return pl.pallas_call(
        kernel,
        out_shape=outs,
        scratch_shapes=[pltpu.VMEM(part, jnp.float32) for part in scratch],
        compiler_params=pltpu.CompilerParams(vmem_limit_bytes=16 * 1024 * 1024),
    )


def gathered(pay, axis, groups):
    count = len(groups[0])
    got = lax.all_to_all(
        pay.reshape(count, -1, LANES), axis, 0, 0, tiled=True, axis_index_groups=groups
    )
    return got.reshape(-1, LANES)


def body(field, conductance, source):
    size_x, size_y = lax.axis_size("gx"), lax.axis_size("gy")
    far_x, far_y = size_x // NEAR_X, size_y // NEAR_Y
    f, c, s = (part.reshape(CELLS, LANES) for part in (field, conductance, source))
    whole, block = shape(CELLS, LANES), (CELLS, LANES)
    everything = jnp.concatenate([f, c, s])
    last, front = call(edges_kernel, (shape(2 * N, LANES), shape(N, LANES)))(everything)
    down = lax.ppermute(last, "gy", [(i, i + 1) for i in range(size_y - 1)])
    following = lax.ppermute(front, "gx", [(i + 1, i) for i in range(size_x - 1)])
    f, c, rhs, gx, nx, mx, mat_x = call(
        lambda *refs: prepare_kernel(size_y, *refs), (whole, whole, whole, whole, whole, whole, shape(3 * N, LANES)), [block]
    )(everything)
    gy, ny, my, mat_y, gz, nz, mz, mat_z = call(
        matrix_kernel,
        (whole, whole, whole, shape(3 * N, LANES), whole, whole, whole)
        + (shape((5 + 2 * len(ROUNDS)) * N, LANES),),
        [block],
    )(c)
    line = shape(N, LANES)
    grx, pay, mat_y, elem_x, gre, ne, me = call(
        lambda *refs: x_forward_kernel(size_y, *refs),
        (whole, shape(NEAR_X * BLOCK, LANES), shape(6 * N, LANES), shape(3 * N, LANES), line, line, line),
        [block, (N, LANES), (N, LANES)],
    )(f, c, rhs, gx, nx, mx, mat_x, mat_y, down, following)
    near = gathered(pay, "gx", [[NEAR_X * i + j for j in range(NEAR_X)] for i in range(far_x)])
    pay = call(lambda *refs: x_merge_kernel(far_x, *refs), shape(far_x * BLOCK, LANES))(near)
    every = gathered(pay, "gx", [[NEAR_X * i + j for i in range(far_x)] for j in range(NEAR_X)])
    ends = (2 * max(far_x, NEAR_X) * N, LANES)
    gry, pay, hr = call(
        lambda *refs: x_back_kernel(far_x, *refs),
        (whole, shape(NEAR_Y * 5 * N, LANES), shape(N, LANES)),
        [block, ends, ends, (N, LANES)],
    )(near, every, elem_x, f, grx, nx, mx, gre, ne, me, gy, ny, my, mat_y)
    near = gathered(pay, "gy", [[NEAR_Y * i + j for j in range(NEAR_Y)] for i in range(far_y)])
    pay = call(lambda *refs: y_merge_kernel(far_y, *refs), shape(far_y * 5 * N, LANES))(near)
    every = gathered(pay, "gy", [[NEAR_Y * i + j for i in range(far_y)] for j in range(NEAR_Y)])
    out = call(
        lambda *refs: y_back_kernel(far_y, *refs), whole, [block, (2 * max(far_y, NEAR_Y) * N, LANES), block, block]
    )(near, every, mat_y, hr, f, gry, ny, my, gz, nz, mz, mat_z)
    return out.reshape(field.shape)


def solution(mesh):
    spec = P("gx", "gy", None)
    return jax.shard_map(
        body, mesh=mesh, in_specs=(spec, spec, spec), out_specs=spec, check_vma=False
    )
```

```python
import jax
import jax.numpy as jnp
from jax import lax
from jax.experimental import pallas as pl
from jax.experimental.pallas import tpu as pltpu
from jax.sharding import PartitionSpec as P

N = 16
CELLS = N * N
LANES = 128
SEGMENTS = LANES // N
ROUNDS = (1, 2, 4)
NEAR_X = 8
BLOCK = 7 * N + 8
NEAR_Y = 4


def rows(k):
    return pl.ds(N * k, N)


def turned(k):
    return pl.ds(k, N, stride=N)


def row(k):
    return pl.ds(k, 1)


def shape(*dims):
    return jax.ShapeDtypeStruct(dims, jnp.float32)


def eliminated(cells, g_ref, n_ref, m_ref, at=rows):
    one = jnp.ones_like(cells[0])
    half = [None] + [0.25 * (cells[k - 1] + cells[k]) for k in range(1, N)]
    first, excess, excess_first = half[1], one, one
    for k in range(1, N - 1):
        g = 1.0 / (first + half[k + 1] + excess)
        n = first * g
        m = half[k + 1] * g
        g_ref[at(k), :] = g
        n_ref[at(k), :] = n
        m_ref[at(k + 1), :] = m
        excess_first = excess_first + n * excess
        first = m * first
        excess = one + m * excess
    return first, excess_first, excess


def forward(right, g_ref, n_ref, m_ref, gr_ref, at=rows):
    r0, carried = right(0), None
    for k in range(1, N):
        carried = right(k) if carried is None else right(k) + m_ref[at(k), :] * carried
        if k < N - 1:
            r0 = r0 + n_ref[at(k), :] * carried
            gr_ref[at(k), :] = g_ref[at(k), :] * carried
    return r0, carried


def backward(u0, u1, gr_ref, n_ref, m_ref, emit, at=rows):
    emit(0, u0)
    emit(N - 1, u1)
    later = u1
    for k in range(N - 2, 0, -1):
        later = gr_ref[at(k), :] + n_ref[at(k), :] * u0 + m_ref[at(k + 1), :] * later
        emit(k, later)


def join_blocks(left, right):
    ql, e0l, e1l, c0l, c1l, r0l, r1l = left
    qr, e0r, e1r, c0r, c1r, r0r, r1r = right
    face = 0.25 * (c1l + c0r)
    h = 1.0 / (ql + face + e1l)
    s, t = face * h, ql * h
    p = s * ql
    ew = e0r + s * e1l
    rw = r0r + s * r1l
    k = 1.0 / (qr + p + ew)
    qk, pk = qr * k, p * k
    joined = (
        qk * p, e0l + t * e1l + pk * ew, e1r + qk * ew, c0l, c1r, r0l + t * r1l + pk * rw, r1r + qk * rw
    )

    def expand(u0, u1):
        w = k * rw + qk * u1 + pk * u0
        return (u0, h * r1l + t * u0 + s * w), (w, u1)

    return joined, expand


def join_elements(left, right):
    kl, eal, ebl, ral, rbl = left
    kr, ear, ebr, rar, rbr = right
    em, rm = ebl + ear, rbl + rar
    k = 1.0 / (kl + kr + em)
    lk, rk = kl * k, kr * k
    joined = (lk * kr, eal + lk * em, ebr + rk * em, ral + lk * rm, rbr + rk * rm)

    def expand(u0, u1):
        middle = k * rm + lk * u0 + rk * u1
        return (u0, middle), (middle, u1)

    return joined, expand


def tree(parts, join):
    levels = []
    while len(parts) > 1:
        pairs = [join(parts[i], parts[i + 1]) for i in range(0, len(parts), 2)]
        levels.append([expand for _, expand in pairs])
        parts = [joined for joined, _ in pairs]

    def ends(u0, u1):
        found = [(u0, u1)]
        for expands in reversed(levels):
            found = [end for expand, both in zip(expands, found) for end in expand(*both)]
        return found

    return parts[0], ends


def chosen(found, scratch_ref, index, count=N):
    for i, (u0, u1) in enumerate(found):
        scratch_ref[pl.ds(2 * N * i, count), :] = u0
        scratch_ref[pl.ds(2 * N * i + N, count), :] = u1
    start = pl.multiple_of(index * 2 * N, 2 * N)
    return scratch_ref[pl.ds(start, count), :], scratch_ref[pl.ds(start + N, count), :]


def parts_of(ref, i, count):
    return tuple(ref[rows(count * i + k), :] for k in range(count))


def replicate(pay_ref, values, copies):
    for i in range(copies):
        for k, value in enumerate(values):
            pay_ref[rows(len(values) * i + k), :] = value


def block_of(ref, i):
    return tuple(ref[pl.ds(BLOCK * i + N * k, N), :] for k in range(7))


def extra_of(ref, i):
    return tuple(ref[row(BLOCK * i + 7 * N + k), :] for k in range(7))


def replicate_blocks(pay_ref, values, extra, copies):
    for i in range(copies):
        for k, value in enumerate(values):
            pay_ref[pl.ds(BLOCK * i + N * k, N), :] = value
        for k, value in enumerate(extra + (jnp.zeros_like(extra[0]),)):
            pay_ref[row(BLOCK * i + 7 * N + k), :] = value


def edges_kernel(all_ref, last_ref):
    for at in (0, 1):
        last_ref[rows(at), :] = all_ref[pl.ds(CELLS * at + N - 1, N, stride=N), :]


def prepare_kernel(size_y, all_ref, s_ref, f_ref, c_ref, rhs_ref, g_ref, n_ref, m_ref, mat_ref, ay_ref):
    f_ref[...] = all_ref[pl.ds(0, CELLS), :]
    c_ref[...] = all_ref[pl.ds(CELLS, CELLS), :]
    cells = [all_ref[rows(N + k), :] for k in range(N)]
    for k, part in enumerate(eliminated(cells, g_ref, n_ref, m_ref)):
        mat_ref[rows(k), :] = part
    flux = None
    for y in range(N - 1):
        c0, c1 = c_ref[turned(y), :], c_ref[turned(y + 1), :]
        f0, f1 = f_ref[turned(y), :], f_ref[turned(y + 1), :]
        after = 0.5 * (c0 + c1) * (f1 - f0)
        ay_ref[turned(y), :] = after if flux is None else after - flux
        flux = after
    top = lax.axis_index("gy") == size_y - 1
    ay_ref[turned(N - 1), :] = -flux - jnp.where(top, 0.5 * c1 * f1, 0.0)
    lane = lax.broadcasted_iota(jnp.int32, (N, LANES), 1)
    for k in range(N):
        c, f = cells[k], f_ref[rows(k), :]
        c_next = jnp.where(lane < LANES - 1, pltpu.roll(c, LANES - 1, 1), 0.0)
        f_next = jnp.where(lane < LANES - 1, pltpu.roll(f, LANES - 1, 1), 0.0)
        upper = 0.5 * (c + c_next) * (f_next - f)
        lower = jnp.where(lane > 0, pltpu.roll(upper, 1, 1), 0.5 * c * f)
        rhs_ref[rows(k), :] = 2.0 * f + s_ref[rows(k), :] + ay_ref[rows(k), :] + (upper - lower)


def x_forward_kernel(
    size_y, f_ref, c_ref, rhs_ref, g_ref, n_ref, m_ref, mat_ref, maty_ref, down_ref, gr_ref, pay_ref, elem_ref, gre_ref, ne_ref, me_ref, r_ref, ge_ref, flux_ref
):
    r_ref[...] = rhs_ref[...]
    first, last, below = c_ref[turned(0), :], c_ref[turned(N - 1), :], down_ref[rows(1), :]
    flux = 0.5 * (below + first) * (f_ref[turned(0), :] - down_ref[rows(0), :])
    r_ref[turned(0), :] = r_ref[turned(0), :] - flux
    flux_ref[...] = flux
    r0, r1 = forward(lambda k: r_ref[rows(k), :], g_ref, n_ref, m_ref, gr_ref)
    values = parts_of(mat_ref, 0, 3) + (c_ref[rows(0), :], c_ref[rows(N - 1), :], r0, r1)
    cells = [down_ref[row(N + k), :] for k in range(N)]
    extra = eliminated(cells, ge_ref, ne_ref, me_ref, row) + (cells[0], cells[N - 1])
    extra += forward(lambda k: flux_ref[row(k), :], ge_ref, ne_ref, me_ref, gre_ref, row)
    replicate_blocks(pay_ref, values, extra, NEAR_X)
    q, e0, e1 = parts_of(maty_ref, 0, 3)
    e1 = e1 + jnp.where(lax.axis_index("gy") == size_y - 1, 0.25 * last, 0.0)
    face = 0.25 * (below + first)
    h = 1.0 / (q + face + e0)
    qh, fh = q * h, face * h
    replicate(elem_ref, (qh * face, fh * e0, e1 + qh * e0, qh, fh, h), 1)


def x_merge_kernel(far, got_ref, pay_ref):
    whole, _ = tree([block_of(got_ref, i) for i in range(NEAR_X)], join_blocks)
    extra, _ = tree([extra_of(got_ref, i) for i in range(NEAR_X)], join_blocks)
    replicate_blocks(pay_ref, whole, extra, far)


def segment(value, s, up):
    return pltpu.roll(value, N - s if up else s, 0)


def matrix_kernel(
    c_ref, g_ref, n_ref, m_ref, mat_ref, gz_ref, nz_ref, mz_ref, matz_ref, cz_ref
):
    cells = [c_ref[turned(k), :] for k in range(N)]
    for k, part in enumerate(eliminated(cells, g_ref, n_ref, m_ref)):
        mat_ref[rows(k), :] = part
    turn(c_ref, cz_ref)
    cells = [cz_ref[turned(k), :] for k in range(N)]
    q, e0, e1 = eliminated(cells, gz_ref, nz_ref, mz_ref)
    place = lax.broadcasted_iota(jnp.int32, (N, LANES), 0) % SEGMENTS
    inside_low, inside_high = place > 0, place < SEGMENTS - 1
    c0, c1 = cells[0], cells[N - 1]
    low = 0.25 * (jnp.where(inside_low, segment(c1, 1, False), 0.0) + c0)
    high = 0.25 * (jnp.where(inside_high, segment(c0, 1, True), 0.0) + c1)
    e0 = e0 + jnp.where(inside_low, 0.0, low)
    e1 = e1 + jnp.where(inside_high, 0.0, high)
    low = jnp.where(inside_low, low, 0.0)
    high = jnp.where(inside_high, high, 0.0)
    h = 1.0 / (q + high + e1)
    qh, eh = q * h, e1 * h
    lower = low * segment(qh, 1, False)
    upper = qh * high
    excess = e0 + q * eh + low * segment(eh, 1, False)
    parts = [h, qh, high * h, low]
    for s in ROUNDS:
        g = 1.0 / (lower + upper + excess)
        before, after = lower * segment(g, s, False), upper * segment(g, s, True)
        parts += [before, after]
        excess = excess + before * segment(excess, s, False) + after * segment(excess, s, True)
        lower, upper = before * segment(lower, s, False), after * segment(upper, s, True)
    for k, part in enumerate(parts + [1.0 / excess]):
        matz_ref[rows(k), :] = part


def turn(from_ref, to_ref):
    for half in range(CELLS // LANES):
        part = pl.ds(LANES * half, LANES)
        to_ref[part, :] = from_ref[part, :].T


def x_ends(far, near_ref, all_ref, part_of, ends_ref, count):
    me = lax.axis_index("gx")
    whole, ends = tree([part_of(all_ref, i) for i in range(far)], join_blocks)
    q, e0, e1, c0, c1, r0, r1 = whole
    e0, e1 = e0 + 0.25 * c0, e1 + 0.25 * c1
    h = 1.0 / (q + e1)
    qh = q * h
    u0 = (r0 + qh * r1) / (e0 + qh * e1)
    u0, u1 = chosen(ends(u0, h * r1 + qh * u0), ends_ref, me // NEAR_X, count)
    _, ends = tree([part_of(near_ref, i) for i in range(NEAR_X)], join_blocks)
    return chosen(ends(u0, u1), ends_ref, me % NEAR_X, count)


def x_back_kernel(
    far, near_ref, all_ref, f_ref, gr_ref, n_ref, m_ref, gre_ref, ne_ref, me_ref, gy_ref, ny_ref, my_ref, mat_ref, gry_ref, pay_ref, hr_ref, u_ref, ends_ref, endse_ref, below_ref
):
    u0, u1 = x_ends(far, near_ref, all_ref, block_of, ends_ref, N)
    v0, v1 = x_ends(far, near_ref, all_ref, extra_of, endse_ref, 1)

    def emit(k, w):
        u_ref[rows(k), :] = w - 2.0 * f_ref[rows(k), :]

    def emit_below(k, w):
        below_ref[row(k), :] = w

    backward(u0, u1, gr_ref, n_ref, m_ref, emit)
    backward(v0, v1, gre_ref, ne_ref, me_ref, emit_below, row)
    r0, r1 = forward(lambda k: u_ref[turned(k), :], gy_ref, ny_ref, my_ref, gry_ref)
    kappa, ea, eb, qh, fh, h = parts_of(mat_ref, 0, 6)
    replicate(pay_ref, (kappa, ea, eb, fh * r0 + below_ref[...], r1 + qh * r0), NEAR_Y)
    hr_ref[...] = h * r0


def y_merge_kernel(far, got_ref, pay_ref):
    whole, _ = tree([parts_of(got_ref, i, 5) for i in range(NEAR_Y)], join_elements)
    replicate(pay_ref, whole, far)


def y_back_kernel(
    far, near_ref, all_ref, mat_ref, hr_ref, f_ref, gry_ref, ny_ref, my_ref, gz_ref, nz_ref, mz_ref, matz_ref, out_ref, u_ref, ends_ref, uz_ref, grz_ref, done_ref, sem
):
    me = lax.axis_index("gy")
    (kappa, _, eb, _, rb), ends = tree([parts_of(all_ref, i, 5) for i in range(far)], join_elements)
    u1 = rb / (kappa + eb)
    u0, u1 = chosen(ends(jnp.zeros_like(u1), u1), ends_ref, me // NEAR_Y)
    _, ends = tree([parts_of(near_ref, i, 5) for i in range(NEAR_Y)], join_elements)
    below, u1 = chosen(ends(u0, u1), ends_ref, me % NEAR_Y)
    u0 = hr_ref[...] + mat_ref[rows(3), :] * u1 + mat_ref[rows(4), :] * below

    def emit_y(k, u):
        u_ref[turned(k), :] = u

    backward(u0, u1, gry_ref, ny_ref, my_ref, emit_y)
    turn(u_ref, uz_ref)
    r0, r1 = forward(lambda k: uz_ref[turned(k), :], gz_ref, nz_ref, mz_ref, grz_ref)
    h, qh, fh, low = parts_of(matz_ref, 0, 4)
    right = r0 + qh * r1 + low * segment(h * r1, 1, False)
    for at, s in enumerate(ROUNDS):
        before, after = matz_ref[rows(4 + 2 * at), :], matz_ref[rows(5 + 2 * at), :]
        right = right + before * segment(right, s, False) + after * segment(right, s, True)
    u0 = right * matz_ref[rows(4 + 2 * len(ROUNDS)), :]
    u1 = h * r1 + qh * u0 + fh * segment(u0, 1, True)

    def emit_z(k, u):
        uz_ref[turned(k), :] = u

    backward(u0, u1, grz_ref, nz_ref, mz_ref, emit_z)
    copies = []
    for half in range(CELLS // LANES):
        part = pl.ds(LANES * half, LANES)
        done_ref[part, :] = f_ref[part, :] + uz_ref[part, :].T
        copies.append(
            pltpu.make_async_copy(done_ref.at[part, :], out_ref.at[part, :], sem.at[half])
        )
        copies[half].start()
    for copy in copies:
        copy.wait()


def call(kernel, outs, scratch=(), **kwargs):
    return pl.pallas_call(
        kernel,
        out_shape=outs,
        scratch_shapes=[
            pltpu.VMEM(part, jnp.float32) if isinstance(part, tuple) else part for part in scratch
        ],
        compiler_params=pltpu.CompilerParams(vmem_limit_bytes=16 * 1024 * 1024),
        **kwargs,
    )


def gathered(pay, axis, groups):
    count = len(groups[0])
    got = lax.all_to_all(
        pay.reshape(count, -1, LANES), axis, 0, 0, tiled=True, axis_index_groups=groups
    )
    return got.reshape(-1, LANES)


def body(field, conductance, source):
    size_x, size_y = lax.axis_size("gx"), lax.axis_size("gy")
    far_x, far_y = size_x // NEAR_X, size_y // NEAR_Y
    f, c, s = (part.reshape(CELLS, LANES) for part in (field, conductance, source))
    whole, block = shape(CELLS, LANES), (CELLS, LANES)
    everything = jnp.concatenate([f, c])
    last = call(edges_kernel, shape(2 * N, LANES))(everything)
    down = lax.ppermute(last, "gy", [(i, i + 1) for i in range(size_y - 1)])
    f, c, rhs, gx, nx, mx, mat_x = call(
        lambda *refs: prepare_kernel(size_y, *refs), (whole, whole, whole, whole, whole, whole, shape(3 * N, LANES)), [block]
    )(everything, s)
    gy, ny, my, mat_y, gz, nz, mz, mat_z = call(
        matrix_kernel,
        (whole, whole, whole, shape(3 * N, LANES), whole, whole, whole)
        + (shape((5 + 2 * len(ROUNDS)) * N, LANES),),
        [block],
    )(c)
    line = shape(N, LANES)
    grx, pay, mat_y, gre, ne, me = call(
        lambda *refs: x_forward_kernel(size_y, *refs),
        (whole, shape(NEAR_X * BLOCK, LANES), shape(6 * N, LANES), line, line, line),
        [block, (N, LANES), (N, LANES)],
    )(f, c, rhs, gx, nx, mx, mat_x, mat_y, down)
    near = gathered(pay, "gx", [[NEAR_X * i + j for j in range(NEAR_X)] for i in range(far_x)])
    pay = call(lambda *refs: x_merge_kernel(far_x, *refs), shape(far_x * BLOCK, LANES))(near)
    every = gathered(pay, "gx", [[NEAR_X * i + j for i in range(far_x)] for j in range(NEAR_X)])
    ends = (2 * max(far_x, NEAR_X) * N, LANES)
    gry, pay, hr = call(
        lambda *refs: x_back_kernel(far_x, *refs),
        (whole, shape(NEAR_Y * 5 * N, LANES), shape(N, LANES)),
        [block, ends, ends, (N, LANES)],
    )(near, every, f, grx, nx, mx, gre, ne, me, gy, ny, my, mat_y)
    near = gathered(pay, "gy", [[NEAR_Y * i + j for j in range(NEAR_Y)] for i in range(far_y)])
    pay = call(lambda *refs: y_merge_kernel(far_y, *refs), shape(far_y * 5 * N, LANES))(near)
    every = gathered(pay, "gy", [[NEAR_Y * i + j for i in range(far_y)] for j in range(NEAR_Y)])
    out = call(
        lambda *refs: y_back_kernel(far_y, *refs), whole,
        [block, (2 * max(far_y, NEAR_Y) * N, LANES), block, block, block, pltpu.SemaphoreType.DMA((2,))],
        out_specs=pl.BlockSpec(memory_space=pl.ANY),
    )(near, every, mat_y, hr, f, gry, ny, my, gz, nz, mz, mat_z)
    return out.reshape(field.shape)


def solution(mesh):
    spec = P("gx", "gy", None)
    return jax.shard_map(
        body, mesh=mesh, in_specs=(spec, spec, spec), out_specs=spec, check_vma=False
    )
```

```python
import jax
import jax.numpy as jnp
from jax import lax
from jax.experimental import pallas as pl
from jax.experimental.pallas import tpu as pltpu
from jax.sharding import PartitionSpec as P

N = 16
CELLS = N * N
LANES = 128
SEGMENTS = LANES // N
ROUNDS = (1, 2, 4)
NEAR_X = 8
BLOCK = 7 * N + 8
NEAR_Y = 4


def rows(k):
    return pl.ds(N * k, N)


def turned(k):
    return pl.ds(k, N, stride=N)


def row(k):
    return pl.ds(k, 1)


def shape(*dims):
    return jax.ShapeDtypeStruct(dims, jnp.float32)


def eliminated(cells, g_ref, n_ref, m_ref, at=rows):
    one = jnp.ones_like(cells[0])
    half = [None] + [0.25 * (cells[k - 1] + cells[k]) for k in range(1, N)]
    first, excess, excess_first = half[1], one, one
    for k in range(1, N - 1):
        g = 1.0 / (first + half[k + 1] + excess)
        n = first * g
        m = half[k + 1] * g
        g_ref[at(k), :] = g
        n_ref[at(k), :] = n
        m_ref[at(k + 1), :] = m
        excess_first = excess_first + n * excess
        first = m * first
        excess = one + m * excess
    return first, excess_first, excess


def forward(right, g_ref, n_ref, m_ref, gr_ref, at=rows):
    r0, carried = right(0), None
    for k in range(1, N):
        carried = right(k) if carried is None else right(k) + m_ref[at(k), :] * carried
        if k < N - 1:
            r0 = r0 + n_ref[at(k), :] * carried
            gr_ref[at(k), :] = g_ref[at(k), :] * carried
    return r0, carried


def backward(u0, u1, gr_ref, n_ref, m_ref, emit, at=rows):
    emit(0, u0)
    emit(N - 1, u1)
    later = u1
    for k in range(N - 2, 0, -1):
        later = gr_ref[at(k), :] + n_ref[at(k), :] * u0 + m_ref[at(k + 1), :] * later
        emit(k, later)


def join_blocks(left, right):
    ql, e0l, e1l, c0l, c1l, r0l, r1l = left
    qr, e0r, e1r, c0r, c1r, r0r, r1r = right
    face = 0.25 * (c1l + c0r)
    h = 1.0 / (ql + face + e1l)
    s, t = face * h, ql * h
    p = s * ql
    ew = e0r + s * e1l
    rw = r0r + s * r1l
    k = 1.0 / (qr + p + ew)
    qk, pk = qr * k, p * k
    joined = (
        qk * p, e0l + t * e1l + pk * ew, e1r + qk * ew, c0l, c1r, r0l + t * r1l + pk * rw, r1r + qk * rw
    )

    def expand(u0, u1):
        w = k * rw + qk * u1 + pk * u0
        return (u0, h * r1l + t * u0 + s * w), (w, u1)

    return joined, expand


def join_elements(left, right):
    kl, eal, ebl, ral, rbl = left
    kr, ear, ebr, rar, rbr = right
    em, rm = ebl + ear, rbl + rar
    k = 1.0 / (kl + kr + em)
    lk, rk = kl * k, kr * k
    joined = (lk * kr, eal + lk * em, ebr + rk * em, ral + lk * rm, rbr + rk * rm)

    def expand(u0, u1):
        middle = k * rm + lk * u0 + rk * u1
        return (u0, middle), (middle, u1)

    return joined, expand


def tree(parts, join):
    levels = []
    while len(parts) > 1:
        pairs = [join(parts[i], parts[i + 1]) for i in range(0, len(parts), 2)]
        levels.append([expand for _, expand in pairs])
        parts = [joined for joined, _ in pairs]

    def ends(u0, u1):
        found = [(u0, u1)]
        for expands in reversed(levels):
            found = [end for expand, both in zip(expands, found) for end in expand(*both)]
        return found

    return parts[0], ends


def chosen(found, scratch_ref, index, count=N):
    for i, (u0, u1) in enumerate(found):
        scratch_ref[pl.ds(2 * N * i, count), :] = u0
        scratch_ref[pl.ds(2 * N * i + N, count), :] = u1
    start = pl.multiple_of(index * 2 * N, 2 * N)
    return scratch_ref[pl.ds(start, count), :], scratch_ref[pl.ds(start + N, count), :]


def parts_of(ref, i, count):
    return tuple(ref[rows(count * i + k), :] for k in range(count))


def replicate(pay_ref, values, copies):
    for i in range(copies):
        for k, value in enumerate(values):
            pay_ref[rows(len(values) * i + k), :] = value


def block_of(ref, i):
    return tuple(ref[pl.ds(BLOCK * i + N * k, N), :] for k in range(7))


def extra_of(ref, i):
    return tuple(ref[row(BLOCK * i + 7 * N + k), :] for k in range(7))


def replicate_blocks(pay_ref, values, extra, copies):
    for i in range(copies):
        for k, value in enumerate(values):
            pay_ref[pl.ds(BLOCK * i + N * k, N), :] = value
        for k, value in enumerate(extra + (jnp.zeros_like(extra[0]),)):
            pay_ref[row(BLOCK * i + 7 * N + k), :] = value


def edges_kernel(all_ref, last_ref):
    for at in (0, 1):
        last_ref[rows(at), :] = all_ref[pl.ds(CELLS * at + N - 1, N, stride=N), :]


def prepare_kernel(size_y, all_ref, s_ref, f_ref, c_ref, rhs_ref, g_ref, n_ref, m_ref, mat_ref, ay_ref):
    f_ref[...] = all_ref[pl.ds(0, CELLS), :]
    c_ref[...] = all_ref[pl.ds(CELLS, CELLS), :]
    cells = [all_ref[rows(N + k), :] for k in range(N)]
    for k, part in enumerate(eliminated(cells, g_ref, n_ref, m_ref)):
        mat_ref[rows(k), :] = part
    flux = None
    for y in range(N - 1):
        c0, c1 = c_ref[turned(y), :], c_ref[turned(y + 1), :]
        f0, f1 = f_ref[turned(y), :], f_ref[turned(y + 1), :]
        after = 0.5 * (c0 + c1) * (f1 - f0)
        ay_ref[turned(y), :] = after if flux is None else after - flux
        flux = after
    top = lax.axis_index("gy") == size_y - 1
    ay_ref[turned(N - 1), :] = -flux - jnp.where(top, 0.5 * c1 * f1, 0.0)
    lane = lax.broadcasted_iota(jnp.int32, (N, LANES), 1)
    for k in range(N):
        c, f = cells[k], f_ref[rows(k), :]
        c_next = jnp.where(lane < LANES - 1, pltpu.roll(c, LANES - 1, 1), 0.0)
        f_next = jnp.where(lane < LANES - 1, pltpu.roll(f, LANES - 1, 1), 0.0)
        upper = 0.5 * (c + c_next) * (f_next - f)
        lower = jnp.where(lane > 0, pltpu.roll(upper, 1, 1), 0.5 * c * f)
        rhs_ref[rows(k), :] = 2.0 * f + s_ref[rows(k), :] + ay_ref[rows(k), :] + (upper - lower)


def x_forward_kernel(
    size_y, f_ref, c_ref, rhs_ref, g_ref, n_ref, m_ref, mat_ref, maty_ref, down_ref, gr_ref, pay_ref, elem_ref, gre_ref, ne_ref, me_ref, r_ref, ge_ref, flux_ref
):
    r_ref[...] = rhs_ref[...]
    first, last, below = c_ref[turned(0), :], c_ref[turned(N - 1), :], down_ref[rows(1), :]
    flux = 0.5 * (below + first) * (f_ref[turned(0), :] - down_ref[rows(0), :])
    r_ref[turned(0), :] = r_ref[turned(0), :] - flux
    flux_ref[...] = flux
    r0, r1 = forward(lambda k: r_ref[rows(k), :], g_ref, n_ref, m_ref, gr_ref)
    values = parts_of(mat_ref, 0, 3) + (c_ref[rows(0), :], c_ref[rows(N - 1), :], r0, r1)
    cells = [down_ref[row(N + k), :] for k in range(N)]
    extra = eliminated(cells, ge_ref, ne_ref, me_ref, row) + (cells[0], cells[N - 1])
    extra += forward(lambda k: flux_ref[row(k), :], ge_ref, ne_ref, me_ref, gre_ref, row)
    replicate_blocks(pay_ref, values, extra, NEAR_X)
    q, e0, e1 = parts_of(maty_ref, 0, 3)
    e1 = e1 + jnp.where(lax.axis_index("gy") == size_y - 1, 0.25 * last, 0.0)
    face = 0.25 * (below + first)
    h = 1.0 / (q + face + e0)
    qh, fh = q * h, face * h
    replicate(elem_ref, (qh * face, fh * e0, e1 + qh * e0, qh, fh, h), 1)


def x_merge_kernel(far, got_ref, pay_ref):
    whole, _ = tree([block_of(got_ref, i) for i in range(NEAR_X)], join_blocks)
    extra, _ = tree([extra_of(got_ref, i) for i in range(NEAR_X)], join_blocks)
    replicate_blocks(pay_ref, whole, extra, far)


def segment(value, s, up):
    return pltpu.roll(value, N - s if up else s, 0)


def matrix_kernel(
    c_ref, g_ref, n_ref, m_ref, mat_ref, gz_ref, nz_ref, mz_ref, matz_ref, cz_ref
):
    cells = [c_ref[turned(k), :] for k in range(N)]
    for k, part in enumerate(eliminated(cells, g_ref, n_ref, m_ref)):
        mat_ref[rows(k), :] = part
    turn(c_ref, cz_ref)
    cells = [cz_ref[turned(k), :] for k in range(N)]
    q, e0, e1 = eliminated(cells, gz_ref, nz_ref, mz_ref)
    place = lax.broadcasted_iota(jnp.int32, (N, LANES), 0) % SEGMENTS
    inside_low, inside_high = place > 0, place < SEGMENTS - 1
    c0, c1 = cells[0], cells[N - 1]
    low = 0.25 * (jnp.where(inside_low, segment(c1, 1, False), 0.0) + c0)
    high = 0.25 * (jnp.where(inside_high, segment(c0, 1, True), 0.0) + c1)
    e0 = e0 + jnp.where(inside_low, 0.0, low)
    e1 = e1 + jnp.where(inside_high, 0.0, high)
    low = jnp.where(inside_low, low, 0.0)
    high = jnp.where(inside_high, high, 0.0)
    h = 1.0 / (q + high + e1)
    qh, eh = q * h, e1 * h
    lower = low * segment(qh, 1, False)
    upper = qh * high
    excess = e0 + q * eh + low * segment(eh, 1, False)
    parts = [h, qh, high * h, low]
    for s in ROUNDS:
        g = 1.0 / (lower + upper + excess)
        before, after = lower * segment(g, s, False), upper * segment(g, s, True)
        parts += [before, after]
        excess = excess + before * segment(excess, s, False) + after * segment(excess, s, True)
        lower, upper = before * segment(lower, s, False), after * segment(upper, s, True)
    for k, part in enumerate(parts + [1.0 / excess]):
        matz_ref[rows(k), :] = part


def setup_kernel(size_y, all_ref, s_ref, *refs):
    prepared, matrices, (ay_ref, cz_ref) = refs[:7], refs[7:15], refs[15:]
    prepare_kernel(size_y, all_ref, s_ref, *prepared, ay_ref)
    matrix_kernel(prepared[1], *matrices, cz_ref)


def turn(from_ref, to_ref):
    for half in range(CELLS // LANES):
        part = pl.ds(LANES * half, LANES)
        to_ref[part, :] = from_ref[part, :].T


def x_ends(far, near_ref, all_ref, part_of, ends_ref, count):
    me = lax.axis_index("gx")
    whole, ends = tree([part_of(all_ref, i) for i in range(far)], join_blocks)
    q, e0, e1, c0, c1, r0, r1 = whole
    e0, e1 = e0 + 0.25 * c0, e1 + 0.25 * c1
    h = 1.0 / (q + e1)
    qh = q * h
    u0 = (r0 + qh * r1) / (e0 + qh * e1)
    u0, u1 = chosen(ends(u0, h * r1 + qh * u0), ends_ref, me // NEAR_X, count)
    _, ends = tree([part_of(near_ref, i) for i in range(NEAR_X)], join_blocks)
    return chosen(ends(u0, u1), ends_ref, me % NEAR_X, count)


def x_back_kernel(
    far, near_ref, all_ref, f_ref, gr_ref, n_ref, m_ref, gre_ref, ne_ref, me_ref, gy_ref, ny_ref, my_ref, mat_ref, gry_ref, pay_ref, hr_ref, u_ref, ends_ref, endse_ref, below_ref
):
    u0, u1 = x_ends(far, near_ref, all_ref, block_of, ends_ref, N)
    v0, v1 = x_ends(far, near_ref, all_ref, extra_of, endse_ref, 1)

    def emit(k, w):
        u_ref[rows(k), :] = w - 2.0 * f_ref[rows(k), :]

    def emit_below(k, w):
        below_ref[row(k), :] = w

    backward(u0, u1, gr_ref, n_ref, m_ref, emit)
    backward(v0, v1, gre_ref, ne_ref, me_ref, emit_below, row)
    r0, r1 = forward(lambda k: u_ref[turned(k), :], gy_ref, ny_ref, my_ref, gry_ref)
    kappa, ea, eb, qh, fh, h = parts_of(mat_ref, 0, 6)
    replicate(pay_ref, (kappa, ea, eb, fh * r0 + below_ref[...], r1 + qh * r0), NEAR_Y)
    hr_ref[...] = h * r0


def y_merge_kernel(far, got_ref, pay_ref):
    whole, _ = tree([parts_of(got_ref, i, 5) for i in range(NEAR_Y)], join_elements)
    replicate(pay_ref, whole, far)


def y_back_kernel(
    far, near_ref, all_ref, mat_ref, hr_ref, f_ref, gry_ref, ny_ref, my_ref, gz_ref, nz_ref, mz_ref, matz_ref, out_ref, u_ref, ends_ref, uz_ref, grz_ref, done_ref, sem
):
    me = lax.axis_index("gy")
    (kappa, _, eb, _, rb), ends = tree([parts_of(all_ref, i, 5) for i in range(far)], join_elements)
    u1 = rb / (kappa + eb)
    u0, u1 = chosen(ends(jnp.zeros_like(u1), u1), ends_ref, me // NEAR_Y)
    _, ends = tree([parts_of(near_ref, i, 5) for i in range(NEAR_Y)], join_elements)
    below, u1 = chosen(ends(u0, u1), ends_ref, me % NEAR_Y)
    u0 = hr_ref[...] + mat_ref[rows(3), :] * u1 + mat_ref[rows(4), :] * below

    def emit_y(k, u):
        u_ref[turned(k), :] = u

    backward(u0, u1, gry_ref, ny_ref, my_ref, emit_y)
    turn(u_ref, uz_ref)
    r0, r1 = forward(lambda k: uz_ref[turned(k), :], gz_ref, nz_ref, mz_ref, grz_ref)
    h, qh, fh, low = parts_of(matz_ref, 0, 4)
    right = r0 + qh * r1 + low * segment(h * r1, 1, False)
    for at, s in enumerate(ROUNDS):
        before, after = matz_ref[rows(4 + 2 * at), :], matz_ref[rows(5 + 2 * at), :]
        right = right + before * segment(right, s, False) + after * segment(right, s, True)
    u0 = right * matz_ref[rows(4 + 2 * len(ROUNDS)), :]
    u1 = h * r1 + qh * u0 + fh * segment(u0, 1, True)

    def emit_z(k, u):
        uz_ref[turned(k), :] = u

    backward(u0, u1, grz_ref, nz_ref, mz_ref, emit_z)
    copies = []
    for half in range(CELLS // LANES):
        part = pl.ds(LANES * half, LANES)
        done_ref[part, :] = f_ref[part, :] + uz_ref[part, :].T
        copies.append(
            pltpu.make_async_copy(done_ref.at[part, :], out_ref.at[part, :], sem.at[half])
        )
        copies[half].start()
    for copy in copies:
        copy.wait()


def call(kernel, outs, scratch=(), **kwargs):
    return pl.pallas_call(
        kernel,
        out_shape=outs,
        scratch_shapes=[
            pltpu.VMEM(part, jnp.float32) if isinstance(part, tuple) else part for part in scratch
        ],
        compiler_params=pltpu.CompilerParams(vmem_limit_bytes=16 * 1024 * 1024),
        **kwargs,
    )


def gathered(pay, axis, groups):
    count = len(groups[0])
    got = lax.all_to_all(
        pay.reshape(count, -1, LANES), axis, 0, 0, tiled=True, axis_index_groups=groups
    )
    return got.reshape(-1, LANES)


def body(field, conductance, source):
    size_x, size_y = lax.axis_size("gx"), lax.axis_size("gy")
    far_x, far_y = size_x // NEAR_X, size_y // NEAR_Y
    f, c, s = (part.reshape(CELLS, LANES) for part in (field, conductance, source))
    whole, block = shape(CELLS, LANES), (CELLS, LANES)
    everything = jnp.concatenate([f, c])
    last = call(edges_kernel, shape(2 * N, LANES))(everything)
    down = lax.ppermute(last, "gy", [(i, i + 1) for i in range(size_y - 1)])
    f, c, rhs, gx, nx, mx, mat_x, gy, ny, my, mat_y, gz, nz, mz, mat_z = call(
        lambda *refs: setup_kernel(size_y, *refs),
        (whole, whole, whole, whole, whole, whole, shape(3 * N, LANES))
        + (whole, whole, whole, shape(3 * N, LANES), whole, whole, whole)
        + (shape((5 + 2 * len(ROUNDS)) * N, LANES),),
        [block, block],
    )(everything, s)
    line = shape(N, LANES)
    grx, pay, mat_y, gre, ne, me = call(
        lambda *refs: x_forward_kernel(size_y, *refs),
        (whole, shape(NEAR_X * BLOCK, LANES), shape(6 * N, LANES), line, line, line),
        [block, (N, LANES), (N, LANES)],
    )(f, c, rhs, gx, nx, mx, mat_x, mat_y, down)
    near = gathered(pay, "gx", [[NEAR_X * i + j for j in range(NEAR_X)] for i in range(far_x)])
    pay = call(lambda *refs: x_merge_kernel(far_x, *refs), shape(far_x * BLOCK, LANES))(near)
    every = gathered(pay, "gx", [[NEAR_X * i + j for i in range(far_x)] for j in range(NEAR_X)])
    ends = (2 * max(far_x, NEAR_X) * N, LANES)
    gry, pay, hr = call(
        lambda *refs: x_back_kernel(far_x, *refs),
        (whole, shape(NEAR_Y * 5 * N, LANES), shape(N, LANES)),
        [block, ends, ends, (N, LANES)],
    )(near, every, f, grx, nx, mx, gre, ne, me, gy, ny, my, mat_y)
    near = gathered(pay, "gy", [[NEAR_Y * i + j for j in range(NEAR_Y)] for i in range(far_y)])
    pay = call(lambda *refs: y_merge_kernel(far_y, *refs), shape(far_y * 5 * N, LANES))(near)
    every = gathered(pay, "gy", [[NEAR_Y * i + j for i in range(far_y)] for j in range(NEAR_Y)])
    out = call(
        lambda *refs: y_back_kernel(far_y, *refs), whole,
        [block, (2 * max(far_y, NEAR_Y) * N, LANES), block, block, block, pltpu.SemaphoreType.DMA((2,))],
        out_specs=pl.BlockSpec(memory_space=pl.ANY),
    )(near, every, mat_y, hr, f, gry, ny, my, gz, nz, mz, mat_z)
    return out.reshape(field.shape)


def solution(mesh):
    spec = P("gx", "gy", None)
    return jax.shard_map(
        body, mesh=mesh, in_specs=(spec, spec, spec), out_specs=spec, check_vma=False
    )
```
